256 devices in a mesh: sub: 32 (over z, y_hi, core), nbr: 8 (over y_lo, x).
Axes of the slice: x: 4, y: 4 (y_hi: 2, y_lo: 2; y = y_hi * 2 + y_lo), z: 8, core: 2. Of those that a mesh axis runs over, the one named last changes fastest.
Arguments:
- eigenvectors: bfloat16 [32, 64, 131072], P('sub', None, 'nbr'), may hold values from -0.3125 to 0.3125
- stencil_coef: float32 [32, 27, 131072], P('sub', None, 'nbr'), may hold values from -1 to 1
- layout: int32 [27], replicated, may hold values from 0 to 26, each once
- band_links: int32 [32, 8], P('sub'), may hold values from 0 to 1, as said below
- send_rows: int32 [32, 8, 8192], P('sub', None, 'nbr'), may hold values from 0 to 16383
- receive_rows: int32 [32, 8, 8192], P('sub', None, 'nbr'), may hold values from 0 to 16383
Outputs:
- diagonal_tiles: float32 [32, 64, 64], P('sub')
- coupling_tiles: float32 [32, 8, 64, 64], P('sub')
The draws below stay inside these ranges and needn't reach their ends.
Inputs may be any that keep to these rules, and one draw needn't show every extreme that they name: band_links[s, o] = band_links[nb(s, o), opp(o)] for every s and o. `send_rows`: each entry indexes a cell within the block of 16384 cells of its group of 1024 entries. `receive_rows`: each entry indexes a cell within the block of 16384 cells of its group of 1024 entries.
All inputs are finite; a program needn't handle non-finite values.
Results may differ from the reference program's by a relative error of at most 0.0029.
Values may be sent and summed in bfloat16 or wider, within the bound.
A program may use at most 64 MiB of HBM per device.

```python
import jax
import jax.numpy as jnp
from jax import lax

K = 64
G = 64
R_DEV = 1024
REACH = 4
SLOTS = 8
SUBS = 32
PL = 32
CELLS_DEV = 16384
CELLS = 131072
ROWS = 8192


def draw_band_links(key, part):
    key = jax.random.fold_in(key, 11)
    forward = jax.random.randint(key, (SUBS, REACH), 0, 2).astype(jnp.int32)
    subdomain = jnp.arange(SUBS, dtype=jnp.int32)[:, None]
    distance = jnp.arange(REACH, dtype=jnp.int32)[None, :]
    source = (subdomain - distance - 1) % SUBS
    backward = forward[source, distance]
    return jnp.concatenate([forward, backward], axis=1).astype(jnp.int32)


def with_ends(entries, rng, low, largest):
    extent = entries.shape
    spot = [jax.random.randint(jax.random.fold_in(rng, axis), (), 0, extent[axis]) for axis in range(len(extent))]
    entries = entries.at[tuple(spot)].set(low)
    longest = extent.index(max(extent))
    spot[longest] = (spot[longest] + 1) % extent[longest]
    return entries.at[tuple(spot)].set(largest)


def level_of(key, dims, cuts, smallest, high):
    factor_of = 1.0
    for position, parts in cuts:
        steps = jax.random.uniform(jax.random.fold_in(jax.random.fold_in(key, 6), position), (parts,), jnp.float32, smallest / len(cuts), high / len(cuts))
        factor_of = factor_of * jnp.repeat(jnp.exp(steps), dims[position] // parts).reshape((-1,) + (1,) * (len(dims) - 1 - position))
    return factor_of


def scatter_about(stream_key, dims, deviation, reach, cuts=(), held_as=jnp.bfloat16):
    result = jax.random.normal(stream_key, dims, jnp.float32) * deviation
    if len(cuts) > 0:
        result = level_of(stream_key, dims, cuts, -0.22, 0.18) * result
    return jnp.clip(result, min=-reach, max=reach).astype(held_as)


def setup_inputs(seed: int = 0) -> dict:
    arg_keys = jax.random.split(jax.random.key(seed), 7)
    eigenvectors = scatter_about(arg_keys[0], (SUBS, K, CELLS), (G * 6) ** -0.5, 0.3125, ((0, 32), (2, 8)))
    stencil_coef = scatter_about(arg_keys[1], (SUBS, 27, CELLS), 0.19, 1.0, ((0, 32), (2, 8)), jnp.float32)
    layout = jax.random.permutation(arg_keys[2], 27).astype(jnp.int32)
    band_links = draw_band_links(jax.random.fold_in(arg_keys[6], 71), 0)
    send_rows = with_ends(jax.random.randint(arg_keys[4], (SUBS, SLOTS, ROWS), 0, CELLS_DEV), jax.random.fold_in(arg_keys[4], 1), 0, CELLS_DEV - 1).astype(jnp.int32)
    receive_rows = with_ends(jax.random.randint(arg_keys[5], (SUBS, SLOTS, ROWS), 0, CELLS_DEV), jax.random.fold_in(arg_keys[5], 1), 0, CELLS_DEV - 1).astype(jnp.int32)
    return {"eigenvectors": eigenvectors, "stencil_coef": stencil_coef, "layout": layout, "band_links": band_links, "send_rows": send_rows, "receive_rows": receive_rows}


def offset_list():
    return [index + 1 for index in range(REACH)] + [-(index + 1) for index in range(REACH)]


def apply_stencil(field_block, weights):
    plane_count = field_block.shape[1]
    padded = jnp.pad(field_block, ((0, 0), (1, 1), (1, 1), (1, 1)))
    summed = jnp.zeros(field_block.shape, jnp.float32)
    number = 0
    for shift_x in (-1, 0, 1):
        for shift_y in (-1, 0, 1):
            for shift_z in (-1, 0, 1):
                window = padded[:, 1 + shift_x:1 + shift_x + plane_count, 1 + shift_y:1 + shift_y + G, 1 + shift_z:1 + shift_z + G]
                summed = summed + weights[number][None] * window.astype(jnp.float32)
                number += 1
    return summed.astype(jnp.bfloat16)


def reference(eigenvectors, stencil_coef, layout, band_links, send_rows, receive_rows):
    slot_count = 2 * REACH
    offsets = offset_list()
    block_base = ((jnp.arange(ROWS, dtype=jnp.int32) // R_DEV) * CELLS_DEV).astype(jnp.int32)

    def one_subdomain(pieces):
        field_block, coef_block, send_block, receive_block = pieces
        shaped = field_block.reshape(K, PL, G, G)
        weights = coef_block[layout].reshape(27, PL, G, G)
        applied = apply_stencil(shaped, weights).reshape(K, CELLS)
        diagonal_tile = lax.dot_general(field_block, applied, (((1,), (1,)), ((), ())), preferred_element_type=jnp.float32)
        panel = jnp.take(field_block, (send_block + block_base[None]).astype(jnp.int32), axis=1)
        applied_rows = jnp.take(applied, (receive_block + block_base[None]).astype(jnp.int32), axis=1)
        return diagonal_tile, jnp.moveaxis(panel, 1, 0), jnp.moveaxis(applied_rows, 1, 0)

    diagonal_tiles, panels, applied_rows = lax.map(one_subdomain, (eigenvectors, stencil_coef, send_rows, receive_rows))
    tile_list = []
    for index in range(slot_count):
        opposite = (index + REACH) % slot_count
        partner = jnp.roll(panels[:, opposite], -offsets[index], axis=0)
        tile_list.append(jnp.einsum("skr,spr->skp", applied_rows[:, index].astype(jnp.float32), partner.astype(jnp.float32), precision=lax.Precision.HIGHEST))
    tiles = jnp.stack(tile_list, axis=1)
    mirror_list = []
    for index in range(slot_count):
        opposite = (index + REACH) % slot_count
        mirror_list.append(jnp.swapaxes(jnp.roll(tiles[:, opposite], -offsets[index], axis=0), -1, -2))
    mirror = jnp.stack(mirror_list, axis=1)
    coupling_tiles = band_links[:, :, None, None].astype(jnp.float32) * (tiles + mirror)
    return diagonal_tiles, coupling_tiles
```

```python
import functools

import jax
import jax.numpy as jnp
from jax import lax
from jax.experimental import pallas as pl
from jax.experimental.pallas import tpu as pltpu
from jax.sharding import PartitionSpec as P

MESH = pl.DeviceIdType.MESH
G = 64
LANES = 128
PLANE = G * G
PLANE_TILES = PLANE // LANES
WIDE = 256
UNROLL = 16
NT = (((1,), (1,)), ((), ()))
TN = (((0,), (0,)), ((), ()))


def slot_offset(slot):
    back = slot // 4
    return (slot + 1) * (1 - back) + (3 - slot) * back


def kernel(
    subs, nbrs, slots, cells,
    eig, coef, layout, links, send, recv,
    diag_out, coup_out,
    field, wide_field, half_field, table, weights, stored, ident, rows, panel, arrived, owned,
    applied, diagonal, parts_out, parts_in, mirror_out, mirror_in, gathered,
    load_sem, halo_send, halo_recv, panel_send, panel_recv,
    part_send, part_recv, mirror_send, mirror_recv, gather_send, gather_recv,
):
    s = lax.axis_index("sub")
    n = lax.axis_index("nbr")
    pairs = panel.shape[1]
    vectors = field.shape[0]
    tiles = cells // LANES
    opposite_n = (n + slots // 2) % slots

    def neighbour(slot):
        return (s + slot_offset(slot) + subs) % subs

    load_field = pltpu.make_async_copy(
        eig.at[0], field.at[:, pl.ds(PLANE, cells)], load_sem.at[0]
    )
    load_weights = pltpu.make_async_copy(coef.at[0], weights, load_sem.at[1])
    load_field.start()
    load_weights.start()

    barrier = pltpu.get_barrier_semaphore()
    for slot in range(slots):
        pl.semaphore_signal(
            barrier, inc=1, device_id=(neighbour(slot), n), device_id_type=MESH
        )
    for step in range(1, nbrs):
        pl.semaphore_signal(
            barrier, inc=1, device_id=(s, (n + step) % nbrs), device_id_type=MESH
        )
    pl.semaphore_signal(
        barrier, inc=1, device_id=(neighbour(n), opposite_n), device_id_type=MESH
    )

    lane = lax.broadcasted_iota(jnp.int32, (1, LANES), 1)
    low_half = lane < G
    ident[...] = (
        lax.broadcasted_iota(jnp.int32, (WIDE, WIDE), 0)
        == lax.broadcasted_iota(jnp.int32, (WIDE, WIDE), 1)
    ).astype(jnp.float32).astype(jnp.bfloat16)
    diagonal[...] = jnp.zeros_like(diagonal)
    parts_out[...] = jnp.zeros_like(parts_out)

    load_field.wait()
    pl.semaphore_wait(barrier, slots + nbrs)

    last = field.shape[1] - PLANE
    halo_up = pltpu.make_async_remote_copy(
        src_ref=field.at[:, pl.ds(last - PLANE, PLANE)],
        dst_ref=field.at[:, pl.ds(0, PLANE)],
        send_sem=halo_send.at[0],
        recv_sem=halo_recv.at[0],
        device_id=(s, (n + 1) % nbrs),
        device_id_type=MESH,
    )
    halo_down = pltpu.make_async_remote_copy(
        src_ref=field.at[:, pl.ds(PLANE, PLANE)],
        dst_ref=field.at[:, pl.ds(last, PLANE)],
        send_sem=halo_send.at[1],
        recv_sem=halo_recv.at[1],
        device_id=(s, (n + nbrs - 1) % nbrs),
        device_id_type=MESH,
    )

    @pl.when(n < nbrs - 1)
    def _():
        halo_up.start()

    @pl.when(n > 0)
    def _():
        halo_down.start()

    def turn_field(i, carry):
        begin = pl.multiple_of(i * WIDE, WIDE)
        block = field[:, pl.ds(pl.multiple_of(PLANE + begin, WIDE), WIDE)]
        doubled = jnp.concatenate([block, block], axis=0)
        table[pl.ds(begin, WIDE), :] = lax.dot_general(
            ident[...], doubled, NT, preferred_element_type=jnp.float32
        )
        return carry

    lax.fori_loop(0, cells // WIDE, turn_field, 0)

    def gather_rows(index_ref, slot, target):
        def some(i, carry):
            base = pl.multiple_of(i * UNROLL, UNROLL)
            for u in range(UNROLL):
                first = index_ref[0, slot, base + u]
                second = index_ref[0, slot, base + u + pairs]
                rows[pl.ds(base + u, 1), :] = jnp.where(
                    low_half, table[pl.ds(first, 1), :], table[pl.ds(second, 1), :]
                )
            return carry

        lax.fori_loop(0, pairs // UNROLL, some, 0)
        target[slot] = rows[...].astype(jnp.bfloat16)

    def panel_copy(slot, landing):
        return pltpu.make_async_remote_copy(
            src_ref=panel.at[slot],
            dst_ref=arrived.at[landing],
            send_sem=panel_send.at[slot],
            recv_sem=panel_recv.at[landing],
            device_id=(neighbour(slot), n),
            device_id_type=MESH,
        )

    for slot in (1, 5, 0, 4, 2, 6, 3, 7):
        gather_rows(send, slot, panel)
        panel_copy(slot, (slot + slots // 2) % slots).start()

    @pl.when(n > 0)
    def _():
        halo_up.wait_recv()

    @pl.when(n == 0)
    def _():
        field[:, pl.ds(0, PLANE)] = jnp.zeros((vectors, PLANE), jnp.bfloat16)

    @pl.when(n < nbrs - 1)
    def _():
        halo_down.wait_recv()

    @pl.when(n == nbrs - 1)
    def _():
        field[:, pl.ds(last, PLANE)] = jnp.zeros((vectors, PLANE), jnp.bfloat16)

    def widen(i, before):
        value = field[:, pl.ds(pl.multiple_of(i * LANES, LANES), LANES)].astype(jnp.float32)
        turned = pltpu.roll(value, G, 1)
        wide_field[i] = value
        half_field[i] = jnp.where(low_half, before, turned)
        return turned

    field_tiles = field.shape[1] // LANES
    after = lax.fori_loop(
        0, field_tiles, widen, jnp.zeros((vectors, LANES), jnp.float32)
    )
    half_field[field_tiles] = after
    load_weights.wait()

    def stencil(t, carry):
        row = t % PLANE_TILES
        begin = pl.multiple_of(t * LANES, LANES)
        column = lane % G
        column_ok = {-1: column != G - 1, 0: None, 1: column != 0}
        row_ok = {
            -1: (lane + row * LANES) >= G,
            0: None,
            1: (lane + row * LANES) < PLANE - G,
        }
        stored[...] = weights[:, pl.ds(begin, LANES)]
        scaled = []
        for k in range(27):
            b, c = k // 3 % 3 - 1, k % 3 - 1
            w = stored[pl.ds(layout[k], 1), :]
            w = jnp.broadcast_to(w, (8, LANES))
            if c == -1:
                w = pltpu.roll(w, LANES - 1, 1)
            if c == 1:
                w = pltpu.roll(w, 1, 1)
            masks = [m for m in (column_ok[c], row_ok[b]) if m is not None]
            if masks:
                w = jnp.where(functools.reduce(jnp.logical_and, masks), w, 0.0)
            scaled.append(w)
        for pair in range(vectors // 16):
            halves = []
            for half in range(2):
                at = pl.ds(pair * 16 + half * 8, 8)
                sums = [None, None, None]
                for a in range(3):
                    tile = t + a * PLANE_TILES
                    for b in range(3):
                        if b == 1:
                            x = wide_field[tile, at, :]
                        else:
                            x = half_field[tile + b // 2, at, :]
                        for c in range(3):
                            term = scaled[9 * a + 3 * b + c] * x
                            sums[c] = term if sums[c] is None else sums[c] + term
                halves.append(
                    sums[1] + pltpu.roll(sums[0], 1, 1) + pltpu.roll(sums[2], LANES - 1, 1)
                )
            applied[pl.ds(pair * 16, 16), pl.ds(begin, LANES)] = jnp.concatenate(
                halves, axis=0
            ).astype(jnp.bfloat16)
        return carry

    lax.fori_loop(0, tiles, stencil, 0)

    def turn_applied(i, carry):
        begin = pl.multiple_of(i * WIDE, WIDE)
        block = applied[:, pl.ds(begin, WIDE)]
        doubled = jnp.concatenate([block, block], axis=0)
        table[pl.ds(begin, WIDE), :] = lax.dot_general(
            ident[...], doubled, NT, preferred_element_type=jnp.float32
        )
        diagonal[...] += lax.dot_general(
            field[:, pl.ds(pl.multiple_of(PLANE + begin, WIDE), WIDE)],
            doubled, NT, preferred_element_type=jnp.float32,
        )
        return carry

    lax.fori_loop(0, cells // WIDE, turn_applied, 0)

    half = G // 2
    share = half // nbrs
    packed = jnp.where(low_half, diagonal[0:half, :], diagonal[half:G, :])
    for other in range(nbrs):
        parts_out[other, half:half + share, :] = packed[other * share:(other + 1) * share]

    def tile_part(slot):
        gather_rows(recv, slot, owned)
        panel_copy((slot + slots // 2) % slots, slot).wait_recv()
        product = lax.dot_general(
            owned[slot], arrived[slot], TN, preferred_element_type=jnp.float32
        )
        tile = product[0:G] + pltpu.roll(product[G:2 * G], G, 1)
        return jnp.where(low_half, tile[0:half], pltpu.roll(tile[half:G], G, 1))

    def part_copy(other, me):
        return pltpu.make_async_remote_copy(
            src_ref=parts_out.at[other],
            dst_ref=parts_in.at[me],
            send_sem=part_send.at[other],
            recv_sem=part_recv.at[me],
            device_id=(s, other),
            device_id_type=MESH,
        )

    def one_part(step, carry):
        other = (n + step) % nbrs
        parts_out[other, 0:half, :] = tile_part(other)
        part_copy(other, n).start()
        return carry

    lax.fori_loop(1, nbrs, one_part, 0)
    parts_out[n, 0:half, :] = tile_part(n)
    parts_in[n] = parts_out[n]

    def await_part(step, carry):
        other = (n + step) % nbrs
        part_copy(other, other).wait_recv()
        return carry

    lax.fori_loop(1, nbrs, await_part, 0)
    total = parts_in[0]
    for other in range(1, nbrs):
        total = total + parts_in[other]
    mirror_out[...] = total[0:half]
    mirror = pltpu.make_async_remote_copy(
        src_ref=mirror_out,
        dst_ref=mirror_in,
        send_sem=mirror_send,
        recv_sem=mirror_recv,
        device_id=(neighbour(n), opposite_n),
        device_id_type=MESH,
    )
    mirror.start()
    mirror.wait_recv()
    other_tile = mirror_in[...]
    turned_tile = pltpu.roll(other_tile, G, 1)
    square = jnp.concatenate([other_tile, turned_tile, other_tile, turned_tile], axis=0).T
    flipped = jnp.where(low_half, square[0:half], square[half:G])
    link = links[0, n].astype(jnp.float32)
    gathered[n, 0:half, :] = link * (total[0:half] + flipped)
    gathered[n, half:, :] = total[half:]

    def gather_copy(place, other):
        return pltpu.make_async_remote_copy(
            src_ref=gathered.at[place],
            dst_ref=gathered.at[place],
            send_sem=gather_send.at[other],
            recv_sem=gather_recv.at[place],
            device_id=(s, other),
            device_id_type=MESH,
        )

    def send_result(step, carry):
        gather_copy(n, (n + step) % nbrs).start()
        return carry

    def await_result(step, carry):
        other = (n + step) % nbrs
        gather_copy(other, other).wait_recv()
        return carry

    lax.fori_loop(1, nbrs, send_result, 0)
    lax.fori_loop(1, nbrs, await_result, 0)
    for other in range(nbrs):
        value = gathered[other]
        turned = pltpu.roll(value, G, 1)
        coup_out[0, other, 0:half, :] = value[0:half, 0:G]
        coup_out[0, other, half:G, :] = turned[0:half, 0:G]
        at = other * share
        diag_out[0, at:at + share, :] = value[half:half + share, 0:G]
        diag_out[0, half + at:half + at + share, :] = turned[half:half + share, 0:G]

    @pl.when(n < nbrs - 1)
    def _():
        halo_up.wait_send()

    @pl.when(n > 0)
    def _():
        halo_down.wait_send()

    for slot in range(slots):
        panel_copy(slot, (slot + slots // 2) % slots).wait_send()

    def await_sends(step, carry):
        other = (n + step) % nbrs
        part_copy(other, n).wait_send()
        gather_copy(n, other).wait_send()
        return carry

    lax.fori_loop(1, nbrs, await_sends, 0)
    mirror.wait_send()


def body(subs, nbrs, eigenvectors, stencil_coef, layout, band_links, send_rows, receive_rows):
    _, vectors, cells = eigenvectors.shape
    slots, entries = send_rows.shape[1:]
    pairs = entries // 2
    padded = cells + 2 * PLANE
    half = G // 2
    anywhere = pl.BlockSpec(memory_space=pl.ANY)
    smem = pl.BlockSpec(memory_space=pltpu.SMEM)
    vmem = pl.BlockSpec(memory_space=pltpu.VMEM)
    bf16, f32 = jnp.bfloat16, jnp.float32
    dma = pltpu.SemaphoreType.DMA
    return pl.pallas_call(
        functools.partial(kernel, subs, nbrs, slots, cells),
        out_shape=(
            jax.ShapeDtypeStruct((1, G, G), f32),
            jax.ShapeDtypeStruct((1, slots, G, G), f32),
        ),
        in_specs=[anywhere, anywhere, smem, smem, smem, smem],
        out_specs=(vmem, vmem),
        scratch_shapes=[
            pltpu.VMEM((vectors, padded), bf16),
            pltpu.VMEM((padded // LANES, vectors, LANES), f32),
            pltpu.VMEM((padded // LANES + 1, vectors, LANES), f32),
            pltpu.VMEM((cells, LANES), f32),
            pltpu.VMEM((27, cells), f32),
            pltpu.VMEM((27, LANES), f32),
            pltpu.VMEM((WIDE, WIDE), bf16),
            pltpu.VMEM((pairs, LANES), f32),
            pltpu.VMEM((slots, pairs, LANES), bf16),
            pltpu.VMEM((slots, pairs, LANES), bf16),
            pltpu.VMEM((slots, pairs, LANES), bf16),
            pltpu.VMEM((vectors, cells), bf16),
            pltpu.VMEM((G, LANES), f32),
            pltpu.VMEM((nbrs, half + 8, LANES), f32),
            pltpu.VMEM((nbrs, half + 8, LANES), f32),
            pltpu.VMEM((half, LANES), f32),
            pltpu.VMEM((half, LANES), f32),
            pltpu.VMEM((nbrs, half + 8, LANES), f32),
            dma((2,)), dma((2,)), dma((2,)), dma((slots,)), dma((slots,)),
            dma((nbrs,)), dma((nbrs,)), dma, dma, dma((nbrs,)), dma((nbrs,)),
        ],
        compiler_params=pltpu.CompilerParams(
            collective_id=0, has_side_effects=True, vmem_limit_bytes=56 << 20
        ),
    )(eigenvectors, stencil_coef, layout, band_links, send_rows, receive_rows)


def solution(mesh):
    in_specs = (
        P("sub", None, "nbr"),
        P("sub", None, "nbr"),
        P(),
        P("sub", None),
        P("sub", None, "nbr"),
        P("sub", None, "nbr"),
    )
    out_specs = (P("sub", None, None), P("sub", None, None, None))
    return jax.shard_map(
        functools.partial(body, mesh.shape["sub"], mesh.shape["nbr"]),
        mesh=mesh, in_specs=in_specs, out_specs=out_specs, check_vma=False,
    )
```

```python
import functools

import jax
import jax.numpy as jnp
from jax import lax
from jax.experimental import pallas as pl
from jax.experimental.pallas import tpu as pltpu
from jax.sharding import PartitionSpec as P

MESH = pl.DeviceIdType.MESH
G = 64
LANES = 128
PLANE = G * G
PLANE_TILES = PLANE // LANES
WIDE = 256
HALF_TILES = PLANE_TILES + 1
TURN_UNROLL = 8
HALO_UNROLL = 4
STENCIL_UNROLL = 4
NT = (((1,), (1,)), ((), ()))
TN = (((0,), (0,)), ((), ()))


def slot_offset(slot):
    back = slot // 4
    return (slot + 1) * (1 - back) + (3 - slot) * back


def kernel(
    subs, nbrs, slots, cells,
    eig, coef, layout, links, send, recv,
    diag_out, coup_out,
    field, wide_field, half_field, table, weights, shifted, rows, panel, arrived,
    applied, diagonal, parts_out, parts_in, mirror_out, mirror_in, gathered,
    load_sem, halo_send, halo_recv, panel_send, panel_recv,
    part_send, part_recv, mirror_send, mirror_recv, gather_send, gather_recv,
):
    s = lax.axis_index("sub")
    n = lax.axis_index("nbr")
    pairs = panel.shape[1]
    vectors = field.shape[0]
    tiles = cells // LANES
    opposite_n = (n + slots // 2) % slots

    def neighbour(slot):
        return (s + slot_offset(slot) + subs) % subs

    load_field = pltpu.make_async_copy(
        eig.at[0], field.at[:, pl.ds(PLANE, cells)], load_sem.at[0]
    )
    load_weights = pltpu.make_async_copy(coef.at[0], weights, load_sem.at[1])
    load_field.start()
    load_weights.start()

    barrier = pltpu.get_barrier_semaphore()
    for slot in range(slots):
        pl.semaphore_signal(
            barrier, inc=1, device_id=(neighbour(slot), n), device_id_type=MESH
        )
    for step in range(1, nbrs):
        pl.semaphore_signal(
            barrier, inc=1, device_id=(s, (n + step) % nbrs), device_id_type=MESH
        )
    pl.semaphore_signal(
        barrier, inc=1, device_id=(neighbour(n), opposite_n), device_id_type=MESH
    )

    lane = lax.broadcasted_iota(jnp.int32, (1, LANES), 1)
    low_half = lane < G
    diagonal[...] = jnp.zeros_like(diagonal)
    parts_out[...] = jnp.zeros_like(parts_out)

    load_field.wait()
    pl.semaphore_wait(barrier, slots + nbrs)

    last = field.shape[1] - PLANE
    halo_up = pltpu.make_async_remote_copy(
        src_ref=field.at[:, pl.ds(last - PLANE, PLANE)],
        dst_ref=field.at[:, pl.ds(0, PLANE)],
        send_sem=halo_send.at[0],
        recv_sem=halo_recv.at[0],
        device_id=(s, (n + 1) % nbrs),
        device_id_type=MESH,
    )
    halo_down = pltpu.make_async_remote_copy(
        src_ref=field.at[:, pl.ds(PLANE, PLANE)],
        dst_ref=field.at[:, pl.ds(last, PLANE)],
        send_sem=halo_send.at[1],
        recv_sem=halo_recv.at[1],
        device_id=(s, (n + nbrs - 1) % nbrs),
        device_id_type=MESH,
    )

    @pl.when(n < nbrs - 1)
    def _():
        halo_up.start()

    @pl.when(n > 0)
    def _():
        halo_down.start()

    def turn(source, begin, place):
        block = source[:, pl.ds(begin, LANES)].astype(jnp.float32)
        table[pl.ds(place, LANES), :] = jnp.concatenate([block, block], axis=0).T

    def turn_field(i, carry):
        for u in range(TURN_UNROLL):
            begin = pl.multiple_of((i * TURN_UNROLL + u) * LANES, LANES)
            turn(field, pl.multiple_of(PLANE + begin, LANES), begin)
        return carry

    lax.fori_loop(0, tiles // TURN_UNROLL, turn_field, 0)

    def gather_some(index_ref, slot, base):
        first = index_ref.at[0, slot, pl.ds(base, LANES)]
        second = index_ref.at[0, slot, pl.ds(pl.multiple_of(base + pairs, LANES), LANES)]
        for u in range(LANES):
            rows[pl.ds(base + u, 1), :] = jnp.where(
                low_half, table[pl.ds(first[u], 1), :], table[pl.ds(second[u], 1), :]
            )

    column = lane % G
    chunks = pairs // LANES
    per_chunk = tiles // (slots * chunks)

    def widen(tile, source, before):
        value = field[:, pl.ds(pl.multiple_of(source * LANES, LANES), LANES)].astype(jnp.float32)
        turned = pltpu.roll(value, G, 1)
        wide_field[source] = value
        half_field[tile] = jnp.where(low_half, before, turned)
        return turned

    def prepare_weights(tile):
        w = weights[:, pl.ds(pl.multiple_of(tile * LANES, LANES), LANES)]
        shifted[0, tile] = jnp.where(column != G - 1, pltpu.roll(w, LANES - 1, 1), 0.0)
        shifted[1, tile] = w
        shifted[2, tile] = jnp.where(column != 0, pltpu.roll(w, 1, 1), 0.0)

    def panel_copy(slot, landing):
        return pltpu.make_async_remote_copy(
            src_ref=panel.at[slot],
            dst_ref=arrived.at[landing],
            send_sem=panel_send.at[slot],
            recv_sem=panel_recv.at[landing],
            device_id=(neighbour(slot), n),
            device_id_type=MESH,
        )

    blank = jnp.zeros((vectors, LANES), jnp.float32)
    load_weights.wait()
    before = blank
    for position, slot in enumerate((1, 5, 0, 4, 2, 6, 3, 7)):

        def send_chunk(i, before, position=position, slot=slot):
            gather_some(send, slot, pl.multiple_of(i * LANES, LANES))
            group = position * chunks + i
            tile = group * per_chunk
            place = tile // PLANE_TILES * HALF_TILES + tile % PLANE_TILES + HALF_TILES
            before = jnp.where(tile % PLANE_TILES == 0, blank, before)
            for u in range(per_chunk):
                prepare_weights(tile + u)
                before = widen(place + u, tile + u + PLANE_TILES, before)
            half_field[place + per_chunk] = jnp.where(low_half, before, 0.0)
            return before

        before = lax.fori_loop(0, chunks, send_chunk, before)
        panel[slot] = rows[...].astype(jnp.bfloat16)
        panel_copy(slot, (slot + slots // 2) % slots).start()

    @pl.when(n > 0)
    def _():
        halo_up.wait_recv()

    @pl.when(n == 0)
    def _():
        field[:, pl.ds(0, PLANE)] = jnp.zeros((vectors, PLANE), jnp.bfloat16)

    @pl.when(n < nbrs - 1)
    def _():
        halo_down.wait_recv()

    @pl.when(n == nbrs - 1)
    def _():
        field[:, pl.ds(last, PLANE)] = jnp.zeros((vectors, PLANE), jnp.bfloat16)

    halo_planes = (0, field.shape[1] // PLANE - 1)

    def widen_halo(i, carry):
        carry = list(carry)
        for which, plane in enumerate(halo_planes):
            for u in range(HALO_UNROLL):
                t = i * HALO_UNROLL + u
                carry[which] = widen(
                    plane * HALF_TILES + t, plane * PLANE_TILES + t, carry[which]
                )
        return tuple(carry)

    ends = lax.fori_loop(0, PLANE_TILES // HALO_UNROLL, widen_halo, (blank, blank))
    for plane, end in zip(halo_planes, ends):
        half_field[plane * HALF_TILES + PLANE_TILES] = jnp.where(low_half, end, 0.0)
    applied[:, 0:STENCIL_UNROLL * LANES] = jnp.zeros(
        (vectors, STENCIL_UNROLL * LANES), jnp.bfloat16
    )

    def stencil_tile(t):
        plane = t // PLANE_TILES
        scaled = [
            jnp.broadcast_to(shifted[k % 3, t, pl.ds(layout[k], 1), :], (8, LANES))
            for k in range(27)
        ]
        for pair in range(vectors // 16):
            halves = []
            for side in range(2):
                at = pl.ds(pair * 16 + side * 8, 8)
                sums = [None, None, None]
                for a in range(3):
                    for b in range(3):
                        if b == 1:
                            x = wide_field[t + a * PLANE_TILES, at, :]
                        else:
                            x = half_field[t + plane + a * HALF_TILES + b // 2, at, :]
                        for c in range(3):
                            term = scaled[9 * a + 3 * b + c] * x
                            sums[c] = term if sums[c] is None else sums[c] + term
                halves.append(
                    sums[1] + pltpu.roll(sums[0], 1, 1) + pltpu.roll(sums[2], LANES - 1, 1)
                )
            applied[pl.ds(pair * 16, 16), pl.ds(pl.multiple_of(t * LANES, LANES), LANES)] = (
                jnp.concatenate(halves, axis=0).astype(jnp.bfloat16)
            )

    def use_applied(first_tile):
        for u in range(STENCIL_UNROLL):
            begin = pl.multiple_of((first_tile + u) * LANES, LANES)
            turn(applied, begin, begin)
        for u in range(STENCIL_UNROLL // 2):
            begin = pl.multiple_of((first_tile + 2 * u) * LANES, WIDE)
            block = applied[:, pl.ds(begin, WIDE)]
            diagonal[...] += lax.dot_general(
                field[:, pl.ds(pl.multiple_of(PLANE + begin, WIDE), WIDE)],
                jnp.concatenate([block, block], axis=0),
                NT, preferred_element_type=jnp.float32,
            )

    def stencil(i, carry):
        use_applied(jnp.maximum(i - 1, 0) * STENCIL_UNROLL)
        for u in range(STENCIL_UNROLL):
            stencil_tile(i * STENCIL_UNROLL + u)
        return carry

    lax.fori_loop(0, tiles // STENCIL_UNROLL, stencil, 0)
    use_applied(tiles - STENCIL_UNROLL)

    half = G // 2
    share = half // nbrs
    packed = jnp.where(low_half, diagonal[0:half, :], diagonal[half:G, :])
    for other in range(nbrs):
        parts_out[other, half:half + share, :] = packed[other * share:(other + 1) * share]

    def tile_part(slot):
        def own_chunk(i, carry):
            gather_some(recv, slot, pl.multiple_of(i * LANES, LANES))
            return carry

        lax.fori_loop(0, chunks, own_chunk, 0)
        panel_copy((slot + slots // 2) % slots, slot).wait_recv()
        product = lax.dot_general(
            rows[...].astype(jnp.bfloat16), arrived[slot], TN, preferred_element_type=jnp.float32
        )
        tile = product[0:G] + pltpu.roll(product[G:2 * G], G, 1)
        return jnp.where(low_half, tile[0:half], pltpu.roll(tile[half:G], G, 1))

    def part_copy(other, me):
        return pltpu.make_async_remote_copy(
            src_ref=parts_out.at[other],
            dst_ref=parts_in.at[me],
            send_sem=part_send.at[other],
            recv_sem=part_recv.at[me],
            device_id=(s, other),
            device_id_type=MESH,
        )

    def one_part(step, carry):
        other = (n + step) % nbrs
        parts_out[other, 0:half, :] = tile_part(other)
        part_copy(other, n).start()
        return carry

    lax.fori_loop(1, nbrs, one_part, 0)
    parts_out[n, 0:half, :] = tile_part(n)
    parts_in[n] = parts_out[n]

    def await_part(step, carry):
        other = (n + step) % nbrs
        part_copy(other, other).wait_recv()
        return carry

    lax.fori_loop(1, nbrs, await_part, 0)
    total = parts_in[0]
    for other in range(1, nbrs):
        total = total + parts_in[other]
    mirror_out[...] = total[0:half]
    mirror = pltpu.make_async_remote_copy(
        src_ref=mirror_out,
        dst_ref=mirror_in,
        send_sem=mirror_send,
        recv_sem=mirror_recv,
        device_id=(neighbour(n), opposite_n),
        device_id_type=MESH,
    )
    mirror.start()
    mirror.wait_recv()
    other_tile = mirror_in[...]
    turned_tile = pltpu.roll(other_tile, G, 1)
    square = jnp.concatenate([other_tile, turned_tile, other_tile, turned_tile], axis=0).T
    flipped = jnp.where(low_half, square[0:half], square[half:G])
    link = links[0, n].astype(jnp.float32)
    gathered[n, 0:half, :] = link * (total[0:half] + flipped)
    gathered[n, half:, :] = total[half:]

    def gather_copy(place, other):
        return pltpu.make_async_remote_copy(
            src_ref=gathered.at[place],
            dst_ref=gathered.at[place],
            send_sem=gather_send.at[other],
            recv_sem=gather_recv.at[place],
            device_id=(s, other),
            device_id_type=MESH,
        )

    def send_result(step, carry):
        gather_copy(n, (n + step) % nbrs).start()
        return carry

    def await_result(step, carry):
        other = (n + step) % nbrs
        gather_copy(other, other).wait_recv()
        return carry

    lax.fori_loop(1, nbrs, send_result, 0)
    lax.fori_loop(1, nbrs, await_result, 0)
    for other in range(nbrs):
        value = gathered[other]
        turned = pltpu.roll(value, G, 1)
        coup_out[0, other, 0:half, :] = value[0:half, 0:G]
        coup_out[0, other, half:G, :] = turned[0:half, 0:G]
        at = other * share
        diag_out[0, at:at + share, :] = value[half:half + share, 0:G]
        diag_out[0, half + at:half + at + share, :] = turned[half:half + share, 0:G]

    @pl.when(n < nbrs - 1)
    def _():
        halo_up.wait_send()

    @pl.when(n > 0)
    def _():
        halo_down.wait_send()

    for slot in range(slots):
        panel_copy(slot, (slot + slots // 2) % slots).wait_send()

    def await_sends(step, carry):
        other = (n + step) % nbrs
        part_copy(other, n).wait_send()
        gather_copy(n, other).wait_send()
        return carry

    lax.fori_loop(1, nbrs, await_sends, 0)
    mirror.wait_send()


def body(subs, nbrs, eigenvectors, stencil_coef, layout, band_links, send_rows, receive_rows):
    _, vectors, cells = eigenvectors.shape
    slots, entries = send_rows.shape[1:]
    pairs = entries // 2
    padded = cells + 2 * PLANE
    half = G // 2
    anywhere = pl.BlockSpec(memory_space=pl.ANY)
    smem = pl.BlockSpec(memory_space=pltpu.SMEM)
    vmem = pl.BlockSpec(memory_space=pltpu.VMEM)
    bf16, f32 = jnp.bfloat16, jnp.float32
    dma = pltpu.SemaphoreType.DMA
    return pl.pallas_call(
        functools.partial(kernel, subs, nbrs, slots, cells),
        out_shape=(
            jax.ShapeDtypeStruct((1, G, G), f32),
            jax.ShapeDtypeStruct((1, slots, G, G), f32),
        ),
        in_specs=[anywhere, anywhere, smem, smem, smem, smem],
        out_specs=(vmem, vmem),
        scratch_shapes=[
            pltpu.VMEM((vectors, padded), bf16),
            pltpu.VMEM((padded // LANES, vectors, LANES), f32),
            pltpu.VMEM((padded // PLANE * HALF_TILES, vectors, LANES), f32),
            pltpu.VMEM((cells, LANES), f32),
            pltpu.VMEM((27, cells), f32),
            pltpu.VMEM((3, cells // LANES, 27, LANES), f32),
            pltpu.VMEM((pairs, LANES), f32),
            pltpu.VMEM((slots, pairs, LANES), bf16),
            pltpu.VMEM((slots, pairs, LANES), bf16),
            pltpu.VMEM((vectors, cells), bf16),
            pltpu.VMEM((G, LANES), f32),
            pltpu.VMEM((nbrs, half + 8, LANES), f32),
            pltpu.VMEM((nbrs, half + 8, LANES), f32),
            pltpu.VMEM((half, LANES), f32),
            pltpu.VMEM((half, LANES), f32),
            pltpu.VMEM((nbrs, half + 8, LANES), f32),
            dma((2,)), dma((2,)), dma((2,)), dma((slots,)), dma((slots,)),
            dma((nbrs,)), dma((nbrs,)), dma, dma, dma((nbrs,)), dma((nbrs,)),
        ],
        compiler_params=pltpu.CompilerParams(
            collective_id=0, has_side_effects=True, vmem_limit_bytes=56 << 20
        ),
    )(eigenvectors, stencil_coef, layout, band_links, send_rows, receive_rows)


def solution(mesh):
    in_specs = (
        P("sub", None, "nbr"),
        P("sub", None, "nbr"),
        P(),
        P("sub", None),
        P("sub", None, "nbr"),
        P("sub", None, "nbr"),
    )
    out_specs = (P("sub", None, None), P("sub", None, None, None))
    return jax.shard_map(
        functools.partial(body, mesh.shape["sub"], mesh.shape["nbr"]),
        mesh=mesh, in_specs=in_specs, out_specs=out_specs, check_vma=False,
    )
```

```python
import functools

import jax
import jax.numpy as jnp
from jax import lax
from jax.experimental import pallas as pl
from jax.experimental.pallas import tpu as pltpu
from jax.sharding import PartitionSpec as P

MESH = pl.DeviceIdType.MESH
G = 64
LANES = 128
PLANE = G * G
PLANE_TILES = PLANE // LANES
WIDE = 256
HALF_TILES = PLANE_TILES + 1
TURN_UNROLL = 8
HALO_UNROLL = 4
STENCIL_UNROLL = 4
NT = (((1,), (1,)), ((), ()))
TN = (((0,), (0,)), ((), ()))


def slot_offset(slot):
    back = slot // 4
    return (slot + 1) * (1 - back) + (3 - slot) * back


def kernel(
    subs, nbrs, slots, cells,
    eig, coef, layout, links, send, recv,
    result,
    field, wide_field, half_field, table, weights, shifted, rows, panel, arrived,
    applied, diagonal, parts_out, parts_in, mirror_in, gathered,
    load_sem, halo_send, halo_recv, panel_send, panel_recv,
    part_send, part_recv, mirror_send, mirror_recv, gather_send, gather_recv,
):
    s = lax.axis_index("sub")
    n = lax.axis_index("nbr")
    pairs = panel.shape[1]
    vectors = field.shape[0]
    tiles = cells // LANES

    def neighbour(slot):
        return (s + slot_offset(slot) + subs) % subs

    load_field = pltpu.make_async_copy(
        eig.at[0], field.at[:, pl.ds(PLANE, cells)], load_sem.at[0]
    )
    load_weights = pltpu.make_async_copy(coef, weights, load_sem.at[1])
    load_field.start()
    load_weights.start()

    barrier = pltpu.get_barrier_semaphore()
    for slot in range(slots):
        pl.semaphore_signal(
            barrier, inc=1, device_id=(neighbour(slot), n), device_id_type=MESH
        )
    for step in range(1, nbrs):
        pl.semaphore_signal(
            barrier, inc=1, device_id=(s, (n + step) % nbrs), device_id_type=MESH
        )
    for other in range(nbrs):
        pl.semaphore_signal(
            barrier, inc=1, device_id=(neighbour(n), other), device_id_type=MESH
        )

    lane = lax.broadcasted_iota(jnp.int32, (1, LANES), 1)
    low_half = lane < G
    diagonal[...] = jnp.zeros_like(diagonal)
    parts_out[...] = jnp.zeros_like(parts_out)

    load_field.wait()
    pl.semaphore_wait(barrier, 2 * slots + nbrs - 1)

    last = field.shape[1] - PLANE
    halo_up = pltpu.make_async_remote_copy(
        src_ref=field.at[:, pl.ds(last - PLANE, PLANE)],
        dst_ref=field.at[:, pl.ds(0, PLANE)],
        send_sem=halo_send.at[0],
        recv_sem=halo_recv.at[0],
        device_id=(s, (n + 1) % nbrs),
        device_id_type=MESH,
    )
    halo_down = pltpu.make_async_remote_copy(
        src_ref=field.at[:, pl.ds(PLANE, PLANE)],
        dst_ref=field.at[:, pl.ds(last, PLANE)],
        send_sem=halo_send.at[1],
        recv_sem=halo_recv.at[1],
        device_id=(s, (n + nbrs - 1) % nbrs),
        device_id_type=MESH,
    )

    @pl.when(n < nbrs - 1)
    def _():
        halo_up.start()

    @pl.when(n > 0)
    def _():
        halo_down.start()

    def turn(source, begin, place):
        block = source[:, pl.ds(begin, LANES)].astype(jnp.float32)
        table[pl.ds(place, LANES), :] = jnp.concatenate([block, block], axis=0).T

    def turn_field(i, carry):
        for u in range(TURN_UNROLL):
            begin = pl.multiple_of((i * TURN_UNROLL + u) * LANES, LANES)
            turn(field, pl.multiple_of(PLANE + begin, LANES), begin)
        return carry

    lax.fori_loop(0, tiles // TURN_UNROLL, turn_field, 0)

    def gather_some(index_ref, slot, base):
        first = index_ref.at[0, slot, pl.ds(base, LANES)]
        second = index_ref.at[0, slot, pl.ds(pl.multiple_of(base + pairs, LANES), LANES)]
        for u in range(LANES):
            rows[pl.ds(base + u, 1), :] = jnp.where(
                low_half, table[pl.ds(first[u], 1), :], table[pl.ds(second[u], 1), :]
            )

    column = lane % G
    chunks = pairs // LANES
    per_chunk = tiles // (slots * chunks)

    def widen(tile, source, before):
        value = field[:, pl.ds(pl.multiple_of(source * LANES, LANES), LANES)].astype(jnp.float32)
        turned = pltpu.roll(value, G, 1)
        wide_field[source] = value
        half_field[tile] = jnp.where(low_half, before, turned)
        return turned

    def prepare_weights(step):
        at = pl.ds(pl.multiple_of(step // 2 * 8, 8), 8)
        first = step % 2 * 13
        for k in range(14):
            w = weights[first + k, at, :]
            shifted[0, first + k, at, :] = jnp.where(
                column != G - 1, pltpu.roll(w, LANES - 1, 1), 0.0
            )
            shifted[1, first + k, at, :] = w
            shifted[2, first + k, at, :] = jnp.where(column != 0, pltpu.roll(w, 1, 1), 0.0)

    def panel_copy(slot, landing):
        return pltpu.make_async_remote_copy(
            src_ref=panel.at[slot],
            dst_ref=arrived.at[landing],
            send_sem=panel_send.at[slot],
            recv_sem=panel_recv.at[landing],
            device_id=(neighbour(slot), n),
            device_id_type=MESH,
        )

    blank = jnp.zeros((vectors, LANES), jnp.float32)
    load_weights.wait()
    before = blank
    for position, slot in enumerate((1, 5, 0, 4, 2, 6, 3, 7)):

        def send_chunk(i, before, position=position, slot=slot):
            gather_some(send, slot, pl.multiple_of(i * LANES, LANES))
            group = position * chunks + i
            prepare_weights(group)
            tile = group * per_chunk
            place = tile // PLANE_TILES * HALF_TILES + tile % PLANE_TILES + HALF_TILES
            before = jnp.where(tile % PLANE_TILES == 0, blank, before)
            for u in range(per_chunk):
                before = widen(place + u, tile + u + PLANE_TILES, before)
            half_field[place + per_chunk] = jnp.where(low_half, before, 0.0)
            return before

        before = lax.fori_loop(0, chunks, send_chunk, before)
        panel[slot] = rows[...].astype(jnp.bfloat16)
        panel_copy(slot, (slot + slots // 2) % slots).start()

    def take_halos():
        @pl.when(n > 0)
        def _():
            halo_up.wait_recv()

        @pl.when(n == 0)
        def _():
            field[:, pl.ds(0, PLANE)] = jnp.zeros((vectors, PLANE), jnp.bfloat16)

        @pl.when(n < nbrs - 1)
        def _():
            halo_down.wait_recv()

        @pl.when(n == nbrs - 1)
        def _():
            field[:, pl.ds(last, PLANE)] = jnp.zeros((vectors, PLANE), jnp.bfloat16)

        halo_planes = (0, field.shape[1] // PLANE - 1)

        def widen_halo(i, carry):
            carry = list(carry)
            for which, plane in enumerate(halo_planes):
                for u in range(HALO_UNROLL):
                    t = i * HALO_UNROLL + u
                    carry[which] = widen(
                        plane * HALF_TILES + t, plane * PLANE_TILES + t, carry[which]
                    )
            return tuple(carry)

        ends = lax.fori_loop(0, PLANE_TILES // HALO_UNROLL, widen_halo, (blank, blank))
        for plane, end in zip(halo_planes, ends):
            half_field[plane * HALF_TILES + PLANE_TILES] = jnp.where(low_half, end, 0.0)
    def stencil_tile(t):
        plane = t // PLANE_TILES
        scaled = [
            jnp.broadcast_to(shifted[k % 3, layout[k], pl.ds(t, 1), :], (8, LANES))
            for k in range(27)
        ]
        for pair in range(vectors // 16):
            halves = []
            for side in range(2):
                at = pl.ds(pair * 16 + side * 8, 8)
                sums = [None, None, None]
                for a in range(3):
                    for b in range(3):
                        if b == 1:
                            x = wide_field[t + a * PLANE_TILES, at, :]
                        else:
                            x = half_field[t + plane + a * HALF_TILES + b // 2, at, :]
                        for c in range(3):
                            term = scaled[9 * a + 3 * b + c] * x
                            sums[c] = term if sums[c] is None else sums[c] + term
                halves.append(
                    sums[1] + pltpu.roll(sums[0], 1, 1) + pltpu.roll(sums[2], LANES - 1, 1)
                )
            applied[pl.ds(pair * 16, 16), pl.ds(pl.multiple_of(t * LANES, LANES), LANES)] = (
                jnp.concatenate(halves, axis=0).astype(jnp.bfloat16)
            )

    def use_applied(first_tile):
        for u in range(STENCIL_UNROLL):
            begin = pl.multiple_of((first_tile + u) * LANES, LANES)
            turn(applied, begin, begin)
        for u in range(STENCIL_UNROLL // 2):
            begin = pl.multiple_of((first_tile + 2 * u) * LANES, WIDE)
            block = applied[:, pl.ds(begin, WIDE)]
            diagonal[...] += lax.dot_general(
                field[:, pl.ds(pl.multiple_of(PLANE + begin, WIDE), WIDE)],
                jnp.concatenate([block, block], axis=0),
                NT, preferred_element_type=jnp.float32,
            )

    def block(step):
        return (step * STENCIL_UNROLL + PLANE_TILES) % tiles

    def stencil(i, carry):
        use_applied(block(jnp.maximum(i - 1, 0)))
        for u in range(STENCIL_UNROLL):
            stencil_tile(block(i) + u)
        return carry

    blocks = tiles // STENCIL_UNROLL
    applied[:, pl.ds(PLANE, STENCIL_UNROLL * LANES)] = jnp.zeros(
        (vectors, STENCIL_UNROLL * LANES), jnp.bfloat16
    )

    def phase(which, carry):
        @pl.when(which == 1)
        def _():
            take_halos()

        begin = which * (blocks // 2)
        return lax.fori_loop(begin, begin + blocks // 2, stencil, carry)

    lax.fori_loop(0, 2, phase, 0)
    use_applied(block(blocks - 1))

    half = G // 2
    share = half // nbrs
    packed = jnp.where(low_half, diagonal[0:half, :], diagonal[half:G, :])
    for other in range(nbrs):
        parts_out[other, half:half + share, :] = packed[other * share:(other + 1) * share]

    def tile_part(slot):
        def own_chunk(i, carry):
            gather_some(recv, slot, pl.multiple_of(i * LANES, LANES))
            return carry

        lax.fori_loop(0, chunks, own_chunk, 0)
        panel_copy((slot + slots // 2) % slots, slot).wait_recv()
        product = lax.dot_general(
            rows[...].astype(jnp.bfloat16), arrived[slot], TN, preferred_element_type=jnp.float32
        )
        tile = product[0:G] + pltpu.roll(product[G:2 * G], G, 1)
        return jnp.where(low_half, tile[0:half], pltpu.roll(tile[half:G], G, 1))

    def part_copy(other, me):
        return pltpu.make_async_remote_copy(
            src_ref=parts_out.at[other],
            dst_ref=parts_in.at[me],
            send_sem=part_send.at[other],
            recv_sem=part_recv.at[me],
            device_id=(s, other),
            device_id_type=MESH,
        )

    def mirror_copy(slot, me):
        return pltpu.make_async_remote_copy(
            src_ref=parts_out.at[slot, pl.ds(0, half), :],
            dst_ref=mirror_in.at[me],
            send_sem=mirror_send.at[slot],
            recv_sem=mirror_recv.at[me],
            device_id=(neighbour(slot), (slot + slots // 2) % slots),
            device_id_type=MESH,
        )

    parts_out[n, 0:half, :] = tile_part(n)
    mirror_copy(n, n).start()
    parts_in[n] = parts_out[n]

    def one_part(step, carry):
        other = (n + step) % nbrs
        parts_out[other, 0:half, :] = tile_part(other)
        part_copy(other, n).start()
        mirror_copy(other, n).start()
        return carry

    lax.fori_loop(1, nbrs, one_part, 0)

    def await_part(step, carry):
        other = (n + step) % nbrs
        part_copy(other, other).wait_recv()
        return carry

    def await_mirror(other, carry):
        mirror_copy(other, other).wait_recv()
        return carry

    lax.fori_loop(1, nbrs, await_part, 0)
    lax.fori_loop(0, nbrs, await_mirror, 0)
    total = parts_in[0]
    other_tile = mirror_in[0]
    for other in range(1, nbrs):
        total = total + parts_in[other]
        other_tile = other_tile + mirror_in[other]
    turned_tile = pltpu.roll(other_tile, G, 1)
    square = jnp.concatenate([other_tile, turned_tile, other_tile, turned_tile], axis=0).T
    flipped = jnp.where(low_half, square[0:half], square[half:G])
    link = links[0, n].astype(jnp.float32)
    gathered[n, 0:half, :] = link * (total[0:half] + flipped)
    gathered[n, half:, :] = total[half:]

    def gather_copy(place, other):
        return pltpu.make_async_remote_copy(
            src_ref=gathered.at[place],
            dst_ref=gathered.at[place],
            send_sem=gather_send.at[other],
            recv_sem=gather_recv.at[place],
            device_id=(s, other),
            device_id_type=MESH,
        )

    def send_result(step, carry):
        gather_copy(n, (n + step) % nbrs).start()
        return carry

    def await_result(step, carry):
        other = (n + step) % nbrs
        gather_copy(other, other).wait_recv()
        return carry

    lax.fori_loop(1, nbrs, send_result, 0)
    lax.fori_loop(1, nbrs, await_result, 0)
    result[...] = gathered[...]

    @pl.when(n < nbrs - 1)
    def _():
        halo_up.wait_send()

    @pl.when(n > 0)
    def _():
        halo_down.wait_send()

    for slot in range(slots):
        panel_copy(slot, (slot + slots // 2) % slots).wait_send()

    def await_sends(step, carry):
        other = (n + step) % nbrs
        part_copy(other, n).wait_send()
        mirror_copy(other, n).wait_send()
        gather_copy(n, other).wait_send()
        return carry

    lax.fori_loop(1, nbrs, await_sends, 0)
    mirror_copy(n, n).wait_send()


def unpack(packed, diag_out, coup_out):
    nbrs = packed.shape[0]
    half = G // 2
    share = half // nbrs
    for other in range(nbrs):
        value = packed[other]
        turned = pltpu.roll(value, G, 1)
        coup_out[0, other, 0:half, :] = value[0:half, 0:G]
        coup_out[0, other, half:G, :] = turned[0:half, 0:G]
        at = other * share
        diag_out[0, at:at + share, :] = value[half:half + share, 0:G]
        diag_out[0, half + at:half + at + share, :] = turned[half:half + share, 0:G]


def body(subs, nbrs, eigenvectors, stencil_coef, layout, band_links, send_rows, receive_rows):
    _, vectors, cells = eigenvectors.shape
    slots, entries = send_rows.shape[1:]
    pairs = entries // 2
    padded = cells + 2 * PLANE
    half = G // 2
    anywhere = pl.BlockSpec(memory_space=pl.ANY)
    smem = pl.BlockSpec(memory_space=pltpu.SMEM)
    vmem = pl.BlockSpec(memory_space=pltpu.VMEM)
    bf16, f32 = jnp.bfloat16, jnp.float32
    dma = pltpu.SemaphoreType.DMA
    packed = pl.pallas_call(
        functools.partial(kernel, subs, nbrs, slots, cells),
        out_shape=jax.ShapeDtypeStruct((nbrs, half + 8, LANES), f32),
        in_specs=[anywhere, anywhere, smem, smem, smem, smem],
        out_specs=vmem,
        scratch_shapes=[
            pltpu.VMEM((vectors, padded), bf16),
            pltpu.VMEM((padded // LANES, vectors, LANES), f32),
            pltpu.VMEM((padded // PLANE * HALF_TILES, vectors, LANES), f32),
            pltpu.VMEM((cells, LANES), f32),
            pltpu.VMEM((27, cells // LANES, LANES), f32),
            pltpu.VMEM((3, 27, cells // LANES, LANES), f32),
            pltpu.VMEM((pairs, LANES), f32),
            pltpu.VMEM((slots, pairs, LANES), bf16),
            pltpu.VMEM((slots, pairs, LANES), bf16),
            pltpu.VMEM((vectors, cells), bf16),
            pltpu.VMEM((G, LANES), f32),
            pltpu.VMEM((nbrs, half + 8, LANES), f32),
            pltpu.VMEM((nbrs, half + 8, LANES), f32),
            pltpu.VMEM((nbrs, half, LANES), f32),
            pltpu.VMEM((nbrs, half + 8, LANES), f32),
            dma((2,)), dma((2,)), dma((2,)), dma((slots,)), dma((slots,)),
            dma((nbrs,)), dma((nbrs,)), dma((slots,)), dma((nbrs,)), dma((nbrs,)), dma((nbrs,)),
        ],
        compiler_params=pltpu.CompilerParams(
            collective_id=0, has_side_effects=True, vmem_limit_bytes=56 << 20
        ),
    )(eigenvectors, stencil_coef.reshape(27, cells // LANES, LANES), layout, band_links, send_rows, receive_rows)
    return pl.pallas_call(
        unpack,
        out_shape=(
            jax.ShapeDtypeStruct((1, G, G), f32),
            jax.ShapeDtypeStruct((1, slots, G, G), f32),
        ),
        in_specs=[vmem],
        out_specs=(vmem, vmem),
    )(packed)


def solution(mesh):
    in_specs = (
        P("sub", None, "nbr"),
        P("sub", None, "nbr"),
        P(),
        P("sub", None),
        P("sub", None, "nbr"),
        P("sub", None, "nbr"),
    )
    out_specs = (P("sub", None, None), P("sub", None, None, None))
    return jax.shard_map(
        functools.partial(body, mesh.shape["sub"], mesh.shape["nbr"]),
        mesh=mesh, in_specs=in_specs, out_specs=out_specs, check_vma=False,
    )
```

```python
import functools

import jax
import jax.numpy as jnp
from jax import lax
from jax.experimental import pallas as pl
from jax.experimental.pallas import tpu as pltpu
from jax.sharding import PartitionSpec as P

MESH = pl.DeviceIdType.MESH
G = 64
LANES = 128
PLANE = G * G
PLANE_TILES = PLANE // LANES
WIDE = 256
HALF_TILES = PLANE_TILES + 1
PREPARE_UNROLL = 8
HALO_UNROLL = 4
STENCIL_UNROLL = 4
GATHER_PARTS = 2
NT = (((1,), (1,)), ((), ()))
TN = (((0,), (0,)), ((), ()))


def slot_offset(slot):
    back = slot // 4
    return (slot + 1) * (1 - back) + (3 - slot) * back


def kernel(
    subs, nbrs, slots, cells,
    eig, coef, layout_in, links_in, send_in, recv_in,
    result,
    field, wide_field, half_field, table, applied_table, weights, shifted, rows, panel, arrived,
    applied, diagonal, parts_out, parts_in, mirror_in, gathered,
    layout, links, send, recv,
    load_sem, halo_send, halo_recv, panel_send, panel_recv,
    part_send, part_recv, mirror_send, mirror_recv, gather_send, gather_recv,
):
    s = lax.axis_index("sub")
    n = lax.axis_index("nbr")
    pairs = panel.shape[1]
    vectors = field.shape[0]
    tiles = cells // LANES
    chunks = pairs // LANES

    def in_order(step):
        pair = step // 2
        late = pair // 2
        return (1 - pair) * (1 - late) + pair * late + step % 2 * (slots // 2)

    def neighbour(slot):
        return (s + slot_offset(slot) + subs) % subs

    load_field = pltpu.make_async_copy(
        eig.at[0], field.at[:, pl.ds(PLANE, cells)], load_sem.at[0]
    )
    load_weights = pltpu.make_async_copy(coef, weights, load_sem.at[1])
    load_scalars = [
        pltpu.make_async_copy(source, target, load_sem.at[2 + i])
        for i, (source, target) in enumerate(
            ((send_in, send), (recv_in, recv), (layout_in, layout), (links_in, links))
        )
    ]
    load_field.start()
    load_scalars[0].start()
    load_weights.start()
    for load in load_scalars[1:]:
        load.start()

    barrier = pltpu.get_barrier_semaphore()
    for slot in range(slots):
        pl.semaphore_signal(
            barrier, inc=1, device_id=(neighbour(slot), n), device_id_type=MESH
        )
    for step in range(1, nbrs):
        pl.semaphore_signal(
            barrier, inc=1, device_id=(s, (n + step) % nbrs), device_id_type=MESH
        )
    for other in range(nbrs):
        pl.semaphore_signal(
            barrier, inc=1, device_id=(neighbour(n), other), device_id_type=MESH
        )

    lane = lax.broadcasted_iota(jnp.int32, (1, LANES), 1)
    low_half = lane < G
    diagonal[...] = jnp.zeros_like(diagonal)
    parts_out[...] = jnp.zeros_like(parts_out)

    pl.semaphore_wait(barrier, 2 * slots + nbrs - 1)

    last = field.shape[1] - PLANE
    halo_up = pltpu.make_async_remote_copy(
        src_ref=eig.at[0, :, pl.ds(cells - PLANE, PLANE)],
        dst_ref=field.at[:, pl.ds(0, PLANE)],
        send_sem=halo_send.at[0],
        recv_sem=halo_recv.at[0],
        device_id=(s, (n + 1) % nbrs),
        device_id_type=MESH,
    )
    halo_down = pltpu.make_async_remote_copy(
        src_ref=eig.at[0, :, pl.ds(0, PLANE)],
        dst_ref=field.at[:, pl.ds(last, PLANE)],
        send_sem=halo_send.at[1],
        recv_sem=halo_recv.at[1],
        device_id=(s, (n + nbrs - 1) % nbrs),
        device_id_type=MESH,
    )

    @pl.when(n < nbrs - 1)
    def _():
        halo_up.start()

    @pl.when(n > 0)
    def _():
        halo_down.start()

    def turn(block, target, place):
        target[pl.ds(place, LANES), :] = jnp.concatenate([block, block], axis=0).T

    def gather_some(index_ref, source, slot, begin, first, count):
        starts = [
            pl.multiple_of(k * LANES + begin, LANES // GATHER_PARTS)
            for k in range(2 * chunks)
        ]
        views = [index_ref.at[0, slot, pl.ds(start, LANES // GATHER_PARTS)] for start in starts]
        for u in range(first, first + count):
            for k in range(chunks):
                rows[pl.ds(begin + (k * LANES + u), 1), :] = jnp.where(
                    low_half,
                    source[pl.ds(views[k][u], 1), :],
                    source[pl.ds(views[k + chunks][u], 1), :],
                )

    column = lane % G
    blank = jnp.zeros((vectors, LANES), jnp.float32)

    def widen(value, source, tile, before):
        turned = pltpu.roll(value, G, 1)
        wide_field[source] = value
        half_field[tile] = jnp.where(low_half, before, turned)
        return turned

    def wide_tile(source):
        begin = pl.multiple_of(source * LANES, LANES)
        return field[:, pl.ds(begin, LANES)].astype(jnp.float32)

    def prepare(i, before):
        tile = i * PREPARE_UNROLL
        before = jnp.where(tile % PLANE_TILES == 0, blank, before)
        place = (tile // PLANE_TILES + 1) * HALF_TILES + tile % PLANE_TILES
        for u in range(PREPARE_UNROLL):
            value = wide_tile(tile + u + PLANE_TILES)
            turn(value, table, pl.multiple_of((tile + u) * LANES, LANES))
            before = widen(value, tile + u + PLANE_TILES, place + u, before)
        half_field[place + PREPARE_UNROLL] = jnp.where(low_half, before, 0.0)
        at = pl.ds(pl.multiple_of(tile, PREPARE_UNROLL), PREPARE_UNROLL)
        for k in range(27):
            w = weights[k, at, :]
            shifted[0, k, at, :] = jnp.where(column != G - 1, pltpu.roll(w, LANES - 1, 1), 0.0)
            shifted[1, k, at, :] = w
            shifted[2, k, at, :] = jnp.where(column != 0, pltpu.roll(w, 1, 1), 0.0)
        return before

    load_field.wait()
    load_weights.wait()
    for load in load_scalars:
        load.wait()
    lax.fori_loop(0, tiles // PREPARE_UNROLL, prepare, blank)

    def panel_copy(slot, landing):
        return pltpu.make_async_remote_copy(
            src_ref=panel.at[slot],
            dst_ref=arrived.at[landing],
            send_sem=panel_send.at[slot],
            recv_sem=panel_recv.at[landing],
            device_id=(neighbour(slot), n),
            device_id_type=MESH,
        )

    def take_halos():
        @pl.when(n > 0)
        def _():
            halo_up.wait_recv()

        @pl.when(n == 0)
        def _():
            field[:, pl.ds(0, PLANE)] = jnp.zeros((vectors, PLANE), jnp.bfloat16)

        @pl.when(n < nbrs - 1)
        def _():
            halo_down.wait_recv()

        @pl.when(n == nbrs - 1)
        def _():
            field[:, pl.ds(last, PLANE)] = jnp.zeros((vectors, PLANE), jnp.bfloat16)

        halo_planes = (0, field.shape[1] // PLANE - 1)

        def widen_halo(i, carry):
            carry = list(carry)
            for which, plane in enumerate(halo_planes):
                for u in range(HALO_UNROLL):
                    t = i * HALO_UNROLL + u
                    source = plane * PLANE_TILES + t
                    carry[which] = widen(
                        wide_tile(source), source, plane * HALF_TILES + t, carry[which]
                    )
            return tuple(carry)

        ends = lax.fori_loop(0, PLANE_TILES // HALO_UNROLL, widen_halo, (blank, blank))
        for plane, end in zip(halo_planes, ends):
            half_field[plane * HALF_TILES + PLANE_TILES] = jnp.where(low_half, end, 0.0)
    def stencil_tile(t):
        plane = t // PLANE_TILES
        scaled = [
            jnp.broadcast_to(shifted[k % 3, layout[k], pl.ds(t, 1), :], (8, LANES))
            for k in range(27)
        ]
        for pair in range(vectors // 16):
            halves = []
            for side in range(2):
                at = pl.ds(pair * 16 + side * 8, 8)
                sums = [None, None, None]
                for a in range(3):
                    for b in range(3):
                        if b == 1:
                            x = wide_field[t + a * PLANE_TILES, at, :]
                        else:
                            x = half_field[t + plane + a * HALF_TILES + b // 2, at, :]
                        for c in range(3):
                            term = scaled[9 * a + 3 * b + c] * x
                            sums[c] = term if sums[c] is None else sums[c] + term
                halves.append(
                    sums[1] + pltpu.roll(sums[0], 1, 1) + pltpu.roll(sums[2], LANES - 1, 1)
                )
            applied[pl.ds(pair * 16, 16), pl.ds(pl.multiple_of(t * LANES, LANES), LANES)] = (
                jnp.concatenate(halves, axis=0).astype(jnp.bfloat16)
            )

    def use_applied(first_tile):
        for u in range(STENCIL_UNROLL):
            begin = pl.multiple_of((first_tile + u) * LANES, LANES)
            turn(applied[:, pl.ds(begin, LANES)].astype(jnp.float32), applied_table, begin)
        for u in range(STENCIL_UNROLL // 2):
            begin = pl.multiple_of((first_tile + 2 * u) * LANES, WIDE)
            block = applied[:, pl.ds(begin, WIDE)]
            diagonal[...] += lax.dot_general(
                field[:, pl.ds(pl.multiple_of(PLANE + begin, WIDE), WIDE)],
                jnp.concatenate([block, block], axis=0),
                NT, preferred_element_type=jnp.float32,
            )

    def block(step):
        return (step * STENCIL_UNROLL + PLANE_TILES) % tiles

    blocks = tiles // STENCIL_UNROLL
    applied[:, pl.ds(PLANE, STENCIL_UNROLL * LANES)] = jnp.zeros(
        (vectors, STENCIL_UNROLL * LANES), jnp.bfloat16
    )
    piece = LANES // GATHER_PARTS

    def one_slot(position, carry):
        slot = in_order(position)

        def one_block(i, carry):
            step = position * GATHER_PARTS + i
            use_applied(block(jnp.maximum(step - 1, 0)))
            begin = pl.multiple_of(i * piece, piece)
            for u in range(STENCIL_UNROLL):
                count = piece // STENCIL_UNROLL
                gather_some(send, table, slot, begin, u * count, count)
                stencil_tile(block(step) + u)
            return carry

        lax.fori_loop(0, GATHER_PARTS, one_block, 0)
        panel[slot] = rows[...].astype(jnp.bfloat16)
        panel_copy(slot, (slot + slots // 2) % slots).start()
        return carry

    def late_block(step, carry):
        use_applied(block(step - 1))
        for u in range(STENCIL_UNROLL):
            stencil_tile(block(step) + u)
        return carry

    lax.fori_loop(0, slots, one_slot, 0)
    take_halos()
    lax.fori_loop(slots * GATHER_PARTS, blocks, late_block, 0)
    use_applied(block(blocks - 1))

    half = G // 2
    share = half // nbrs
    packed = jnp.where(low_half, diagonal[0:half, :], diagonal[half:G, :])
    for other in range(nbrs):
        parts_out[other, half:half + share, :] = packed[other * share:(other + 1) * share]

    def tile_part(slot):
        def own_some(i, carry):
            begin = pl.multiple_of(i * piece, piece)
            gather_some(recv, applied_table, slot, begin, 0, piece)
            return carry

        lax.fori_loop(0, GATHER_PARTS, own_some, 0)
        panel_copy((slot + slots // 2) % slots, slot).wait_recv()
        product = lax.dot_general(
            rows[...].astype(jnp.bfloat16), arrived[slot], TN, preferred_element_type=jnp.float32
        )
        tile = product[0:G] + pltpu.roll(product[G:2 * G], G, 1)
        return jnp.where(low_half, tile[0:half], pltpu.roll(tile[half:G], G, 1))

    def part_copy(other, me):
        return pltpu.make_async_remote_copy(
            src_ref=parts_out.at[other],
            dst_ref=parts_in.at[me],
            send_sem=part_send.at[other],
            recv_sem=part_recv.at[me],
            device_id=(s, other),
            device_id_type=MESH,
        )

    def mirror_copy(slot, me):
        return pltpu.make_async_remote_copy(
            src_ref=parts_out.at[slot, pl.ds(0, half), :],
            dst_ref=mirror_in.at[me],
            send_sem=mirror_send.at[slot],
            recv_sem=mirror_recv.at[me],
            device_id=(neighbour(slot), (slot + slots // 2) % slots),
            device_id_type=MESH,
        )

    def gather_copy(place, other):
        return pltpu.make_async_remote_copy(
            src_ref=gathered.at[place],
            dst_ref=gathered.at[place],
            send_sem=gather_send.at[other],
            recv_sem=gather_recv.at[place],
            device_id=(s, other),
            device_id_type=MESH,
        )

    def send_result(step, carry):
        gather_copy(n, (n + step) % nbrs).start()
        return carry

    def await_result(step, carry):
        other = (n + step) % nbrs
        gather_copy(other, other).wait_recv()
        return carry

    def await_part(step, carry):
        other = (n + step) % nbrs
        part_copy(other, other).wait_recv()
        return carry

    def await_mirror(other, carry):
        mirror_copy(other, other).wait_recv()
        return carry

    def reduce_slot():
        lax.fori_loop(1, nbrs, await_part, 0)
        lax.fori_loop(0, nbrs, await_mirror, 0)
        total = parts_in[0]
        other_tile = mirror_in[0]
        for other in range(1, nbrs):
            total = total + parts_in[other]
            other_tile = other_tile + mirror_in[other]
        turned_tile = pltpu.roll(other_tile, G, 1)
        square = jnp.concatenate(
            [other_tile, turned_tile, other_tile, turned_tile], axis=0
        ).T
        flipped = jnp.where(low_half, square[0:half], square[half:G])
        link = links[0, n].astype(jnp.float32)
        gathered[n, 0:half, :] = link * (total[0:half] + flipped)
        gathered[n, half:, :] = total[half:]
        lax.fori_loop(1, nbrs, send_result, 0)

    def one_part(step, carry):
        slot = in_order(step)
        parts_out[slot, 0:half, :] = tile_part(slot)
        mirror_copy(slot, n).start()

        @pl.when(slot != n)
        def _():
            part_copy(slot, n).start()

        @pl.when(slot == n)
        def _():
            parts_in[n] = parts_out[n]

        return carry

    lax.fori_loop(0, slots, one_part, 0)

    reduce_slot()

    lax.fori_loop(1, nbrs, await_result, 0)
    result[...] = gathered[...]

    @pl.when(n < nbrs - 1)
    def _():
        halo_up.wait_send()

    @pl.when(n > 0)
    def _():
        halo_down.wait_send()

    for slot in range(slots):
        panel_copy(slot, (slot + slots // 2) % slots).wait_send()

    def await_sends(step, carry):
        other = (n + step) % nbrs
        part_copy(other, n).wait_send()
        mirror_copy(other, n).wait_send()
        gather_copy(n, other).wait_send()
        return carry

    lax.fori_loop(1, nbrs, await_sends, 0)
    mirror_copy(n, n).wait_send()


def unpack(packed, diag_out, coup_out):
    nbrs = packed.shape[0]
    half = G // 2
    share = half // nbrs
    for other in range(nbrs):
        value = packed[other]
        turned = pltpu.roll(value, G, 1)
        coup_out[0, other, 0:half, :] = value[0:half, 0:G]
        coup_out[0, other, half:G, :] = turned[0:half, 0:G]
        at = other * share
        diag_out[0, at:at + share, :] = value[half:half + share, 0:G]
        diag_out[0, half + at:half + at + share, :] = turned[half:half + share, 0:G]


def body(subs, nbrs, eigenvectors, stencil_coef, layout, band_links, send_rows, receive_rows):
    _, vectors, cells = eigenvectors.shape
    slots, entries = send_rows.shape[1:]
    pairs = entries // 2
    padded = cells + 2 * PLANE
    half = G // 2
    anywhere = pl.BlockSpec(memory_space=pl.ANY)
    vmem = pl.BlockSpec(memory_space=pltpu.VMEM)
    bf16, f32 = jnp.bfloat16, jnp.float32
    dma = pltpu.SemaphoreType.DMA
    packed = pl.pallas_call(
        functools.partial(kernel, subs, nbrs, slots, cells),
        out_shape=jax.ShapeDtypeStruct((nbrs, half + 8, LANES), f32),
        in_specs=[anywhere] * 6,
        out_specs=vmem,
        scratch_shapes=[
            pltpu.VMEM((vectors, padded), bf16),
            pltpu.VMEM((padded // LANES, vectors, LANES), f32),
            pltpu.VMEM((padded // PLANE * HALF_TILES, vectors, LANES), f32),
            pltpu.VMEM((cells, LANES), f32),
            pltpu.VMEM((cells, LANES), f32),
            pltpu.VMEM((27, cells // LANES, LANES), f32),
            pltpu.VMEM((3, 27, cells // LANES, LANES), f32),
            pltpu.VMEM((pairs, LANES), f32),
            pltpu.VMEM((slots, pairs, LANES), bf16),
            pltpu.VMEM((slots, pairs, LANES), bf16),
            pltpu.VMEM((vectors, cells), bf16),
            pltpu.VMEM((G, LANES), f32),
            pltpu.VMEM((nbrs, half + 8, LANES), f32),
            pltpu.VMEM((nbrs, half + 8, LANES), f32),
            pltpu.VMEM((nbrs, half, LANES), f32),
            pltpu.VMEM((nbrs, half + 8, LANES), f32),
            pltpu.SMEM(layout.shape, jnp.int32),
            pltpu.SMEM(band_links.shape, jnp.int32),
            pltpu.SMEM(send_rows.shape, jnp.int32),
            pltpu.SMEM(receive_rows.shape, jnp.int32),
            dma((6,)), dma((2,)), dma((2,)), dma((slots,)), dma((slots,)),
            dma((nbrs,)), dma((nbrs,)), dma((slots,)), dma((nbrs,)), dma((nbrs,)), dma((nbrs,)),
        ],
        compiler_params=pltpu.CompilerParams(
            collective_id=0, has_side_effects=True, vmem_limit_bytes=56 << 20
        ),
    )(eigenvectors, stencil_coef.reshape(27, cells // LANES, LANES), layout, band_links, send_rows, receive_rows)
    return pl.pallas_call(
        unpack,
        out_shape=(
            jax.ShapeDtypeStruct((1, G, G), f32),
            jax.ShapeDtypeStruct((1, slots, G, G), f32),
        ),
        in_specs=[vmem],
        out_specs=(vmem, vmem),
    )(packed)


def solution(mesh):
    in_specs = (
        P("sub", None, "nbr"),
        P("sub", None, "nbr"),
        P(),
        P("sub", None),
        P("sub", None, "nbr"),
        P("sub", None, "nbr"),
    )
    out_specs = (P("sub", None, None), P("sub", None, None, None))
    return jax.shard_map(
        functools.partial(body, mesh.shape["sub"], mesh.shape["nbr"]),
        mesh=mesh, in_specs=in_specs, out_specs=out_specs, check_vma=False,
    )
```

```python
import functools

import jax
import jax.numpy as jnp
from jax import lax
from jax.experimental import pallas as pl
from jax.experimental.pallas import tpu as pltpu
from jax.sharding import PartitionSpec as P

MESH = pl.DeviceIdType.MESH
G = 64
LANES = 128
PLANE = G * G
PLANE_TILES = PLANE // LANES
WIDE = 256
HALF_TILES = PLANE_TILES + 1
PREPARE_UNROLL = 8
HALO_UNROLL = 4
STENCIL_UNROLL = 4
GATHER_PARTS = 2
NT = (((1,), (1,)), ((), ()))
TN = (((0,), (0,)), ((), ()))


def slot_offset(slot):
    back = slot // 4
    return (slot + 1) * (1 - back) + (3 - slot) * back


def kernel(
    subs, nbrs, slots, cells,
    eig, coef, layout_in, links_in, send_in, recv_in,
    result,
    field, wide_field, half_field, table, applied_table, begun_sums, weights, shifted, rows, panel, arrived,
    applied, diagonal, parts_out, parts_in, mirror_in, gathered,
    layout, links, send, recv,
    load_sem, halo_send, halo_recv, panel_send, panel_recv,
    part_send, part_recv, mirror_send, mirror_recv, gather_send, gather_recv,
):
    s = lax.axis_index("sub")
    n = lax.axis_index("nbr")
    pairs = panel.shape[1]
    vectors = field.shape[0]
    tiles = cells // LANES
    chunks = pairs // LANES

    def in_order(step):
        pair = step // 2
        late = pair // 2
        return (1 - pair) * (1 - late) + pair * late + step % 2 * (slots // 2)

    def neighbour(slot):
        return (s + slot_offset(slot) + subs) % subs

    load_field = pltpu.make_async_copy(
        eig.at[0], field.at[:, pl.ds(PLANE, cells)], load_sem.at[0]
    )
    load_weights = pltpu.make_async_copy(coef, weights, load_sem.at[1])
    load_scalars = [
        pltpu.make_async_copy(source, target, load_sem.at[2 + i])
        for i, (source, target) in enumerate(
            ((send_in, send), (recv_in, recv), (layout_in, layout), (links_in, links))
        )
    ]
    load_field.start()
    load_scalars[0].start()
    load_weights.start()
    for load in load_scalars[1:]:
        load.start()

    barrier = pltpu.get_barrier_semaphore()
    for slot in range(slots):
        pl.semaphore_signal(
            barrier, inc=1, device_id=(neighbour(slot), n), device_id_type=MESH
        )
    for step in range(1, nbrs):
        pl.semaphore_signal(
            barrier, inc=1, device_id=(s, (n + step) % nbrs), device_id_type=MESH
        )
    for other in range(nbrs):
        pl.semaphore_signal(
            barrier, inc=1, device_id=(neighbour(n), other), device_id_type=MESH
        )

    lane = lax.broadcasted_iota(jnp.int32, (1, LANES), 1)
    low_half = lane < G
    diagonal[...] = jnp.zeros_like(diagonal)
    parts_out[...] = jnp.zeros_like(parts_out)

    pl.semaphore_wait(barrier, 2 * slots + nbrs - 1)

    last = field.shape[1] - PLANE
    halo_up = pltpu.make_async_remote_copy(
        src_ref=eig.at[0, :, pl.ds(cells - PLANE, PLANE)],
        dst_ref=field.at[:, pl.ds(0, PLANE)],
        send_sem=halo_send.at[0],
        recv_sem=halo_recv.at[0],
        device_id=(s, (n + 1) % nbrs),
        device_id_type=MESH,
    )
    halo_down = pltpu.make_async_remote_copy(
        src_ref=eig.at[0, :, pl.ds(0, PLANE)],
        dst_ref=field.at[:, pl.ds(last, PLANE)],
        send_sem=halo_send.at[1],
        recv_sem=halo_recv.at[1],
        device_id=(s, (n + nbrs - 1) % nbrs),
        device_id_type=MESH,
    )

    @pl.when(n < nbrs - 1)
    def _():
        halo_up.start()

    @pl.when(n > 0)
    def _():
        halo_down.start()

    def turn(block, target, place):
        target[pl.ds(place, LANES), :] = jnp.concatenate([block, block], axis=0).T

    def gather_some(index_ref, source, slot, begin, span, first, count):
        starts = [
            pl.multiple_of(k * LANES + begin, span)
            for k in range(2 * chunks)
        ]
        views = [index_ref.at[0, slot, pl.ds(start, span)] for start in starts]
        for u in range(first, first + count):
            for k in range(chunks):
                rows[pl.ds(begin + (k * LANES + u), 1), :] = jnp.where(
                    low_half,
                    source[pl.ds(views[k][u], 1), :],
                    source[pl.ds(views[k + chunks][u], 1), :],
                )

    column = lane % G
    blank = jnp.zeros((vectors, LANES), jnp.float32)

    def widen(value, source, tile, before):
        turned = pltpu.roll(value, G, 1)
        wide_field[source] = value
        half_field[tile] = jnp.where(low_half, before, turned)
        return turned

    def wide_tile(source):
        begin = pl.multiple_of(source * LANES, LANES)
        return field[:, pl.ds(begin, LANES)].astype(jnp.float32)

    def prepare(i, before):
        tile = i * PREPARE_UNROLL
        before = jnp.where(tile % PLANE_TILES == 0, blank, before)
        place = (tile // PLANE_TILES + 1) * HALF_TILES + tile % PLANE_TILES
        for u in range(PREPARE_UNROLL):
            value = wide_tile(tile + u + PLANE_TILES)
            turn(value, table, pl.multiple_of((tile + u) * LANES, LANES))
            before = widen(value, tile + u + PLANE_TILES, place + u, before)
        half_field[place + PREPARE_UNROLL] = jnp.where(low_half, before, 0.0)
        at = pl.ds(pl.multiple_of(tile, PREPARE_UNROLL), PREPARE_UNROLL)
        for k in range(27):
            w = weights[layout[k], at, :]
            if k % 3 == 0:
                w = jnp.where(column != G - 1, pltpu.roll(w, LANES - 1, 1), 0.0)
            if k % 3 == 2:
                w = jnp.where(column != 0, pltpu.roll(w, 1, 1), 0.0)
            shifted[k, at, :] = w
        return before

    load_field.wait()
    load_weights.wait()
    for load in load_scalars:
        load.wait()
    lax.fori_loop(0, tiles // PREPARE_UNROLL, prepare, blank)

    def panel_copy(slot, landing):
        return pltpu.make_async_remote_copy(
            src_ref=panel.at[slot],
            dst_ref=arrived.at[landing],
            send_sem=panel_send.at[slot],
            recv_sem=panel_recv.at[landing],
            device_id=(neighbour(slot), n),
            device_id_type=MESH,
        )

    def take_halos():
        @pl.when(n > 0)
        def _():
            halo_up.wait_recv()

        @pl.when(n == 0)
        def _():
            field[:, pl.ds(0, PLANE)] = jnp.zeros((vectors, PLANE), jnp.bfloat16)

        @pl.when(n < nbrs - 1)
        def _():
            halo_down.wait_recv()

        @pl.when(n == nbrs - 1)
        def _():
            field[:, pl.ds(last, PLANE)] = jnp.zeros((vectors, PLANE), jnp.bfloat16)

        halo_planes = (0, field.shape[1] // PLANE - 1)

        def widen_halo(i, carry):
            carry = list(carry)
            for which, plane in enumerate(halo_planes):
                for u in range(HALO_UNROLL):
                    t = i * HALO_UNROLL + u
                    source = plane * PLANE_TILES + t
                    carry[which] = widen(
                        wide_tile(source), source, plane * HALF_TILES + t, carry[which]
                    )
            return tuple(carry)

        ends = lax.fori_loop(0, PLANE_TILES // HALO_UNROLL, widen_halo, (blank, blank))
        for plane, end in zip(halo_planes, ends):
            half_field[plane * HALF_TILES + PLANE_TILES] = jnp.where(low_half, end, 0.0)
    def stencil_tile(t, planes=(0, 1, 2), begun=False, keep=False):
        plane = t // PLANE_TILES
        place = t % begun_sums.shape[0]
        scaled = {
            k: jnp.broadcast_to(shifted[k, pl.ds(t, 1), :], (8, LANES))
            for a in planes
            for k in range(9 * a, 9 * a + 9)
        }
        for pair in range(vectors // 16):
            halves = []
            for side in range(2):
                at = pl.ds(pair * 16 + side * 8, 8)
                sums = [None, None, None]
                for a in planes:
                    for b in range(3):
                        if b == 1:
                            x = wide_field[t + a * PLANE_TILES, at, :]
                        else:
                            x = half_field[t + plane + a * HALF_TILES + b // 2, at, :]
                        for c in range(3):
                            term = scaled[9 * a + 3 * b + c] * x
                            sums[c] = term if sums[c] is None else sums[c] + term
                value = sums[1] + pltpu.roll(sums[0], 1, 1) + pltpu.roll(sums[2], LANES - 1, 1)
                if begun:
                    value = value + begun_sums[place, at, :]
                if keep:
                    begun_sums[place, at, :] = value
                halves.append(value)
            if not keep:
                applied[pl.ds(pair * 16, 16), pl.ds(pl.multiple_of(t * LANES, LANES), LANES)] = (
                    jnp.concatenate(halves, axis=0).astype(jnp.bfloat16)
                )

    def use_applied(first_tile):
        for u in range(STENCIL_UNROLL):
            begin = pl.multiple_of((first_tile + u) * LANES, LANES)
            turn(applied[:, pl.ds(begin, LANES)].astype(jnp.float32), applied_table, begin)
        for u in range(STENCIL_UNROLL // 2):
            begin = pl.multiple_of((first_tile + 2 * u) * LANES, WIDE)
            block = applied[:, pl.ds(begin, WIDE)]
            diagonal[...] += lax.dot_general(
                field[:, pl.ds(pl.multiple_of(PLANE + begin, WIDE), WIDE)],
                jnp.concatenate([block, block], axis=0),
                NT, preferred_element_type=jnp.float32,
            )

    def block(step):
        return (step * STENCIL_UNROLL + PLANE_TILES) % tiles

    blocks = tiles // STENCIL_UNROLL
    applied[:, pl.ds(PLANE, STENCIL_UNROLL * LANES)] = jnp.zeros(
        (vectors, STENCIL_UNROLL * LANES), jnp.bfloat16
    )
    def one_slot(step, carry):
        slot = in_order(step)
        use_applied(block(jnp.maximum(step - 1, 0)))
        count = LANES // STENCIL_UNROLL
        for u in range(STENCIL_UNROLL):
            gather_some(send, table, slot, 0, LANES, u * count, count)
            stencil_tile(block(step) + u)
        panel[slot] = rows[...].astype(jnp.bfloat16)
        panel_copy(slot, (slot + slots // 2) % slots).start()
        return carry

    def later_block(step, carry):
        use_applied(block(step - 1))
        for u in range(STENCIL_UNROLL):
            stencil_tile(block(step) + u)
        return carry

    lax.fori_loop(0, slots, one_slot, 0)
    lax.fori_loop(slots, blocks // 2, later_block, 0)

    def begin_block(planes, step, carry):
        for u in range(STENCIL_UNROLL):
            stencil_tile(block(step) + u, planes, keep=True)
        return carry

    def finish_block(planes, step, carry):
        use_applied(block(step - 1))
        for u in range(STENCIL_UNROLL):
            stencil_tile(block(step) + u, planes, begun=True)
        return carry

    turn_point = blocks // 2 + blocks // 4
    lax.fori_loop(blocks // 2, turn_point, functools.partial(begin_block, (0, 1)), 0)
    lax.fori_loop(turn_point, blocks, functools.partial(begin_block, (1, 2)), 0)
    take_halos()
    lax.fori_loop(blocks // 2, turn_point, functools.partial(finish_block, (2,)), 0)
    lax.fori_loop(turn_point, blocks, functools.partial(finish_block, (0,)), 0)
    use_applied(block(blocks - 1))

    half = G // 2
    share = half // nbrs
    packed = jnp.where(low_half, diagonal[0:half, :], diagonal[half:G, :])
    for other in range(nbrs):
        parts_out[other, half:half + share, :] = packed[other * share:(other + 1) * share]

    def tile_part(slot):
        def own_some(i, carry):
            span = LANES // GATHER_PARTS
            begin = pl.multiple_of(i * span, span)
            gather_some(recv, applied_table, slot, begin, span, 0, span)
            return carry

        lax.fori_loop(0, GATHER_PARTS, own_some, 0)
        panel_copy((slot + slots // 2) % slots, slot).wait_recv()
        product = lax.dot_general(
            rows[...].astype(jnp.bfloat16), arrived[slot], TN, preferred_element_type=jnp.float32
        )
        tile = product[0:G] + pltpu.roll(product[G:2 * G], G, 1)
        return jnp.where(low_half, tile[0:half], pltpu.roll(tile[half:G], G, 1))

    def part_copy(other, me):
        return pltpu.make_async_remote_copy(
            src_ref=parts_out.at[other],
            dst_ref=parts_in.at[me],
            send_sem=part_send.at[other],
            recv_sem=part_recv.at[me],
            device_id=(s, other),
            device_id_type=MESH,
        )

    def mirror_copy(slot, me):
        return pltpu.make_async_remote_copy(
            src_ref=parts_out.at[slot, pl.ds(0, half), :],
            dst_ref=mirror_in.at[me],
            send_sem=mirror_send.at[slot],
            recv_sem=mirror_recv.at[me],
            device_id=(neighbour(slot), (slot + slots // 2) % slots),
            device_id_type=MESH,
        )

    def gather_copy(place, other):
        return pltpu.make_async_remote_copy(
            src_ref=gathered.at[place],
            dst_ref=gathered.at[place],
            send_sem=gather_send.at[other],
            recv_sem=gather_recv.at[place],
            device_id=(s, other),
            device_id_type=MESH,
        )

    def send_result(step, carry):
        gather_copy(n, (n + step) % nbrs).start()
        return carry

    def await_result(step, carry):
        other = (n + step) % nbrs
        gather_copy(other, other).wait_recv()
        return carry

    def await_part(step, carry):
        other = (n + step) % nbrs
        part_copy(other, other).wait_recv()
        return carry

    def await_mirror(other, carry):
        mirror_copy(other, other).wait_recv()
        return carry

    def reduce_slot():
        lax.fori_loop(1, nbrs, await_part, 0)
        lax.fori_loop(0, nbrs, await_mirror, 0)
        total = parts_in[0]
        other_tile = mirror_in[0]
        for other in range(1, nbrs):
            total = total + parts_in[other]
            other_tile = other_tile + mirror_in[other]
        turned_tile = pltpu.roll(other_tile, G, 1)
        square = jnp.concatenate(
            [other_tile, turned_tile, other_tile, turned_tile], axis=0
        ).T
        flipped = jnp.where(low_half, square[0:half], square[half:G])
        link = links[0, n].astype(jnp.float32)
        gathered[n, 0:half, :] = link * (total[0:half] + flipped)
        gathered[n, half:, :] = total[half:]
        lax.fori_loop(1, nbrs, send_result, 0)

    def one_part(step, carry):
        slot = in_order(step)
        parts_out[slot, 0:half, :] = tile_part(slot)
        mirror_copy(slot, n).start()

        @pl.when(slot != n)
        def _():
            part_copy(slot, n).start()

        @pl.when(slot == n)
        def _():
            parts_in[n] = parts_out[n]

        return carry

    lax.fori_loop(0, slots, one_part, 0)

    reduce_slot()

    lax.fori_loop(1, nbrs, await_result, 0)
    result[...] = gathered[...]

    @pl.when(n < nbrs - 1)
    def _():
        halo_up.wait_send()

    @pl.when(n > 0)
    def _():
        halo_down.wait_send()

    for slot in range(slots):
        panel_copy(slot, (slot + slots // 2) % slots).wait_send()

    def await_sends(step, carry):
        other = (n + step) % nbrs
        part_copy(other, n).wait_send()
        mirror_copy(other, n).wait_send()
        gather_copy(n, other).wait_send()
        return carry

    lax.fori_loop(1, nbrs, await_sends, 0)
    mirror_copy(n, n).wait_send()


def unpack(packed, diag_out, coup_out):
    nbrs = packed.shape[0]
    half = G // 2
    share = half // nbrs
    for other in range(nbrs):
        value = packed[other]
        turned = pltpu.roll(value, G, 1)
        coup_out[0, other, 0:half, :] = value[0:half, 0:G]
        coup_out[0, other, half:G, :] = turned[0:half, 0:G]
        at = other * share
        diag_out[0, at:at + share, :] = value[half:half + share, 0:G]
        diag_out[0, half + at:half + at + share, :] = turned[half:half + share, 0:G]


def body(subs, nbrs, eigenvectors, stencil_coef, layout, band_links, send_rows, receive_rows):
    _, vectors, cells = eigenvectors.shape
    slots, entries = send_rows.shape[1:]
    pairs = entries // 2
    padded = cells + 2 * PLANE
    half = G // 2
    anywhere = pl.BlockSpec(memory_space=pl.ANY)
    vmem = pl.BlockSpec(memory_space=pltpu.VMEM)
    bf16, f32 = jnp.bfloat16, jnp.float32
    dma = pltpu.SemaphoreType.DMA
    packed = pl.pallas_call(
        functools.partial(kernel, subs, nbrs, slots, cells),
        out_shape=jax.ShapeDtypeStruct((nbrs, half + 8, LANES), f32),
        in_specs=[anywhere] * 6,
        out_specs=vmem,
        scratch_shapes=[
            pltpu.VMEM((vectors, padded), bf16),
            pltpu.VMEM((padded // LANES, vectors, LANES), f32),
            pltpu.VMEM((padded // PLANE * HALF_TILES, vectors, LANES), f32),
            pltpu.VMEM((cells, LANES), f32),
            pltpu.VMEM((cells, LANES), f32),
            pltpu.VMEM((cells // LANES // 2, vectors, LANES), f32),
            pltpu.VMEM((27, cells // LANES, LANES), f32),
            pltpu.VMEM((27, cells // LANES, LANES), f32),
            pltpu.VMEM((pairs, LANES), f32),
            pltpu.VMEM((slots, pairs, LANES), bf16),
            pltpu.VMEM((slots, pairs, LANES), bf16),
            pltpu.VMEM((vectors, cells), bf16),
            pltpu.VMEM((G, LANES), f32),
            pltpu.VMEM((nbrs, half + 8, LANES), f32),
            pltpu.VMEM((nbrs, half + 8, LANES), f32),
            pltpu.VMEM((nbrs, half, LANES), f32),
            pltpu.VMEM((nbrs, half + 8, LANES), f32),
            pltpu.SMEM(layout.shape, jnp.int32),
            pltpu.SMEM(band_links.shape, jnp.int32),
            pltpu.SMEM(send_rows.shape, jnp.int32),
            pltpu.SMEM(receive_rows.shape, jnp.int32),
            dma((6,)), dma((2,)), dma((2,)), dma((slots,)), dma((slots,)),
            dma((nbrs,)), dma((nbrs,)), dma((slots,)), dma((nbrs,)), dma((nbrs,)), dma((nbrs,)),
        ],
        compiler_params=pltpu.CompilerParams(
            collective_id=0, has_side_effects=True, vmem_limit_bytes=56 << 20
        ),
    )(eigenvectors, stencil_coef.reshape(27, cells // LANES, LANES), layout, band_links, send_rows, receive_rows)
    return pl.pallas_call(
        unpack,
        out_shape=(
            jax.ShapeDtypeStruct((1, G, G), f32),
            jax.ShapeDtypeStruct((1, slots, G, G), f32),
        ),
        in_specs=[vmem],
        out_specs=(vmem, vmem),
    )(packed)


def solution(mesh):
    in_specs = (
        P("sub", None, "nbr"),
        P("sub", None, "nbr"),
        P(),
        P("sub", None),
        P("sub", None, "nbr"),
        P("sub", None, "nbr"),
    )
    out_specs = (P("sub", None, None), P("sub", None, None, None))
    return jax.shard_map(
        functools.partial(body, mesh.shape["sub"], mesh.shape["nbr"]),
        mesh=mesh, in_specs=in_specs, out_specs=out_specs, check_vma=False,
    )
```

```python
import functools

import jax
import jax.numpy as jnp
from jax import lax
from jax.experimental import pallas as pl
from jax.experimental.pallas import tpu as pltpu
from jax.sharding import PartitionSpec as P

MESH = pl.DeviceIdType.MESH
G = 64
LANES = 128
PLANE = G * G
PLANE_TILES = PLANE // LANES
WIDE = 256
HALF_TILES = PLANE_TILES + 1
PREPARE_UNROLL = 8
HALO_UNROLL = 4
STENCIL_UNROLL = 4
NT = (((1,), (1,)), ((), ()))
TN = (((0,), (0,)), ((), ()))


def slot_offset(slot):
    back = slot // 4
    return (slot + 1) * (1 - back) + (3 - slot) * back


def kernel(
    subs, nbrs, slots, cells,
    eig, coef, layout_in, links_in, send_in, recv_in,
    result,
    field, wide_field, half_field, table, applied_table, begun_sums, weights, shifted, rows, panel, arrived,
    applied, diagonal, parts_out, parts_in, mirror_in, gathered,
    layout, links, send, recv,
    load_sem, halo_send, halo_recv, panel_send, panel_recv,
    part_send, part_recv, mirror_send, mirror_recv, gather_send, gather_recv, result_sem,
):
    s = lax.axis_index("sub")
    n = lax.axis_index("nbr")
    pairs = panel.shape[1]
    vectors = field.shape[0]
    tiles = cells // LANES
    chunks = pairs // LANES

    def in_order(step):
        pair = step // 2
        late = pair // 2
        return (1 - pair) * (1 - late) + pair * late + step % 2 * (slots // 2)

    def neighbour(slot):
        return (s + slot_offset(slot) + subs) % subs

    load_field = pltpu.make_async_copy(
        eig.at[0], field.at[:, pl.ds(PLANE, cells)], load_sem.at[0]
    )
    load_weights = pltpu.make_async_copy(coef, weights, load_sem.at[1])
    load_scalars = [
        pltpu.make_async_copy(source, target, load_sem.at[2 + i])
        for i, (source, target) in enumerate(
            ((send_in, send), (recv_in, recv), (layout_in, layout), (links_in, links))
        )
    ]
    load_field.start()
    load_scalars[0].start()
    load_weights.start()
    for load in load_scalars[1:]:
        load.start()

    barrier = pltpu.get_barrier_semaphore()
    for slot in range(slots):
        pl.semaphore_signal(
            barrier, inc=1, device_id=(neighbour(slot), n), device_id_type=MESH
        )
    for step in range(1, nbrs):
        pl.semaphore_signal(
            barrier, inc=1, device_id=(s, (n + step) % nbrs), device_id_type=MESH
        )
    for other in range(nbrs):
        pl.semaphore_signal(
            barrier, inc=1, device_id=(neighbour(n), other), device_id_type=MESH
        )

    lane = lax.broadcasted_iota(jnp.int32, (1, LANES), 1)
    low_half = lane < G
    diagonal[...] = jnp.zeros_like(diagonal)
    parts_out[...] = jnp.zeros_like(parts_out)

    pl.semaphore_wait(barrier, 2 * slots + nbrs - 1)

    last = field.shape[1] - PLANE
    halo_up = pltpu.make_async_remote_copy(
        src_ref=eig.at[0, :, pl.ds(cells - PLANE, PLANE)],
        dst_ref=field.at[:, pl.ds(0, PLANE)],
        send_sem=halo_send.at[0],
        recv_sem=halo_recv.at[0],
        device_id=(s, (n + 1) % nbrs),
        device_id_type=MESH,
    )
    halo_down = pltpu.make_async_remote_copy(
        src_ref=eig.at[0, :, pl.ds(0, PLANE)],
        dst_ref=field.at[:, pl.ds(last, PLANE)],
        send_sem=halo_send.at[1],
        recv_sem=halo_recv.at[1],
        device_id=(s, (n + nbrs - 1) % nbrs),
        device_id_type=MESH,
    )

    @pl.when(n < nbrs - 1)
    def _():
        halo_up.start()

    @pl.when(n > 0)
    def _():
        halo_down.start()

    def turn(block, target, place):
        target[pl.ds(place, LANES), :] = jnp.concatenate([block, block], axis=0).T

    def gather_some(index_ref, source, slot, target, first, count):
        views = [index_ref.at[0, slot, pl.ds(k * LANES, LANES)] for k in range(2 * chunks)]
        for u in range(first, first + count):
            for k in range(chunks):
                target[pl.ds(k * LANES + u, 1), :] = jnp.where(
                    low_half,
                    source[pl.ds(views[k][u], 1), :],
                    source[pl.ds(views[k + chunks][u], 1), :],
                )

    column = lane % G
    blank = jnp.zeros((vectors, LANES), jnp.float32)

    def widen(value, source, tile, before):
        turned = pltpu.roll(value, G, 1)
        wide_field[source] = value
        half_field[tile] = jnp.where(low_half, before, turned)
        return turned

    def wide_tile(source):
        begin = pl.multiple_of(source * LANES, LANES)
        return field[:, pl.ds(begin, LANES)].astype(jnp.float32)

    def prepare(i, before):
        tile = i * PREPARE_UNROLL
        before = jnp.where(tile % PLANE_TILES == 0, blank, before)
        place = (tile // PLANE_TILES + 1) * HALF_TILES + tile % PLANE_TILES
        for u in range(PREPARE_UNROLL):
            value = wide_tile(tile + u + PLANE_TILES)
            turn(value, table, pl.multiple_of((tile + u) * LANES, LANES))
            before = widen(value, tile + u + PLANE_TILES, place + u, before)
        half_field[place + PREPARE_UNROLL] = jnp.where(low_half, before, 0.0)
        at = pl.ds(pl.multiple_of(tile, PREPARE_UNROLL), PREPARE_UNROLL)
        for k in range(27):
            w = weights[layout[k], at, :]
            if k % 3 == 0:
                w = jnp.where(column != G - 1, pltpu.roll(w, LANES - 1, 1), 0.0)
            if k % 3 == 2:
                w = jnp.where(column != 0, pltpu.roll(w, 1, 1), 0.0)
            shifted[k, at, :] = w
        return before

    load_field.wait()
    load_weights.wait()
    for load in load_scalars:
        load.wait()
    lax.fori_loop(0, tiles // PREPARE_UNROLL, prepare, blank)

    def panel_copy(slot, landing):
        return pltpu.make_async_remote_copy(
            src_ref=panel.at[slot],
            dst_ref=arrived.at[landing],
            send_sem=panel_send.at[slot],
            recv_sem=panel_recv.at[landing],
            device_id=(neighbour(slot), n),
            device_id_type=MESH,
        )

    def take_halos():
        @pl.when(n > 0)
        def _():
            halo_up.wait_recv()

        @pl.when(n == 0)
        def _():
            field[:, pl.ds(0, PLANE)] = jnp.zeros((vectors, PLANE), jnp.bfloat16)

        @pl.when(n < nbrs - 1)
        def _():
            halo_down.wait_recv()

        @pl.when(n == nbrs - 1)
        def _():
            field[:, pl.ds(last, PLANE)] = jnp.zeros((vectors, PLANE), jnp.bfloat16)

        halo_planes = (0, field.shape[1] // PLANE - 1)

        def widen_halo(i, carry):
            carry = list(carry)
            for which, plane in enumerate(halo_planes):
                for u in range(HALO_UNROLL):
                    t = i * HALO_UNROLL + u
                    source = plane * PLANE_TILES + t
                    carry[which] = widen(
                        wide_tile(source), source, plane * HALF_TILES + t, carry[which]
                    )
            return tuple(carry)

        ends = lax.fori_loop(0, PLANE_TILES // HALO_UNROLL, widen_halo, (blank, blank))
        for plane, end in zip(halo_planes, ends):
            half_field[plane * HALF_TILES + PLANE_TILES] = jnp.where(low_half, end, 0.0)
    def stencil_tile(t, planes=(0, 1, 2), begun=False, keep=False):
        plane = t // PLANE_TILES
        place = t % begun_sums.shape[0]
        scaled = {
            k: jnp.broadcast_to(shifted[k, pl.ds(t, 1), :], (8, LANES))
            for a in planes
            for k in range(9 * a, 9 * a + 9)
        }
        for pair in range(vectors // 16):
            halves = []
            for side in range(2):
                at = pl.ds(pair * 16 + side * 8, 8)
                sums = [None, None, None]
                for a in planes:
                    for b in range(3):
                        if b == 1:
                            x = wide_field[t + a * PLANE_TILES, at, :]
                        else:
                            x = half_field[t + plane + a * HALF_TILES + b // 2, at, :]
                        for c in range(3):
                            term = scaled[9 * a + 3 * b + c] * x
                            sums[c] = term if sums[c] is None else sums[c] + term
                value = sums[1] + pltpu.roll(sums[0], 1, 1) + pltpu.roll(sums[2], LANES - 1, 1)
                if begun:
                    value = value + begun_sums[place, at, :]
                if keep:
                    begun_sums[place, at, :] = value
                halves.append(value)
            if not keep:
                applied[pl.ds(pair * 16, 16), pl.ds(pl.multiple_of(t * LANES, LANES), LANES)] = (
                    jnp.concatenate(halves, axis=0).astype(jnp.bfloat16)
                )

    def use_applied(first_tile):
        for u in range(STENCIL_UNROLL):
            begin = pl.multiple_of((first_tile + u) * LANES, LANES)
            turn(applied[:, pl.ds(begin, LANES)].astype(jnp.float32), applied_table, begin)
        for u in range(STENCIL_UNROLL // 2):
            begin = pl.multiple_of((first_tile + 2 * u) * LANES, WIDE)
            block = applied[:, pl.ds(begin, WIDE)]
            diagonal[...] += lax.dot_general(
                field[:, pl.ds(pl.multiple_of(PLANE + begin, WIDE), WIDE)],
                jnp.concatenate([block, block], axis=0),
                NT, preferred_element_type=jnp.float32,
            )

    def block(step):
        return (step * STENCIL_UNROLL + PLANE_TILES) % tiles

    blocks = tiles // STENCIL_UNROLL
    applied[:, pl.ds(PLANE, STENCIL_UNROLL * LANES)] = jnp.zeros(
        (vectors, STENCIL_UNROLL * LANES), jnp.bfloat16
    )
    def one_slot(step, carry):
        slot = in_order(step)
        use_applied(block(jnp.maximum(step - 1, 0)))
        count = LANES // STENCIL_UNROLL
        for u in range(STENCIL_UNROLL):
            gather_some(send, table, slot, rows.at[0], u * count, count)
            stencil_tile(block(step) + u)
        panel[slot] = rows[0].astype(jnp.bfloat16)
        panel_copy(slot, (slot + slots // 2) % slots).start()
        return carry

    def later_block(step, carry):
        use_applied(block(step - 1))
        for u in range(STENCIL_UNROLL):
            stencil_tile(block(step) + u)
        return carry

    lax.fori_loop(0, slots, one_slot, 0)
    lax.fori_loop(slots, blocks // 2, later_block, 0)

    def begin_block(planes, step, carry):
        for u in range(STENCIL_UNROLL):
            stencil_tile(block(step) + u, planes, keep=True)
        return carry

    def finish_block(planes, step, carry):
        use_applied(block(step - 1))
        for u in range(STENCIL_UNROLL):
            stencil_tile(block(step) + u, planes, begun=True)
        return carry

    turn_point = blocks // 2 + blocks // 4
    lax.fori_loop(blocks // 2, turn_point, functools.partial(begin_block, (0, 1)), 0)
    lax.fori_loop(turn_point, blocks, functools.partial(begin_block, (1, 2)), 0)
    take_halos()
    lax.fori_loop(blocks // 2, turn_point, functools.partial(finish_block, (2,)), 0)
    lax.fori_loop(turn_point, blocks, functools.partial(finish_block, (0,)), 0)
    use_applied(block(blocks - 1))

    half = G // 2
    share = half // nbrs
    packed = jnp.where(low_half, diagonal[0:half, :], diagonal[half:G, :])
    for other in range(nbrs):
        parts_out[other, half:half + share, :] = packed[other * share:(other + 1) * share]

    def own_rows(step):
        gather_some(recv, applied_table, in_order(step), rows.at[step % 2], 0, LANES)

    def tile_part(slot, own):
        product = lax.dot_general(
            own.astype(jnp.bfloat16), arrived[slot], TN, preferred_element_type=jnp.float32
        )
        tile = product[0:G] + pltpu.roll(product[G:2 * G], G, 1)
        return jnp.where(low_half, tile[0:half], pltpu.roll(tile[half:G], G, 1))

    def part_copy(other, me):
        return pltpu.make_async_remote_copy(
            src_ref=parts_out.at[other],
            dst_ref=parts_in.at[me],
            send_sem=part_send.at[other],
            recv_sem=part_recv.at[me],
            device_id=(s, other),
            device_id_type=MESH,
        )

    def mirror_copy(slot, me):
        return pltpu.make_async_remote_copy(
            src_ref=parts_out.at[slot, pl.ds(0, half), :],
            dst_ref=mirror_in.at[me],
            send_sem=mirror_send.at[slot],
            recv_sem=mirror_recv.at[me],
            device_id=(neighbour(slot), (slot + slots // 2) % slots),
            device_id_type=MESH,
        )

    def gather_copy(place, other):
        return pltpu.make_async_remote_copy(
            src_ref=gathered.at[place],
            dst_ref=gathered.at[place],
            send_sem=gather_send.at[other],
            recv_sem=gather_recv.at[place],
            device_id=(s, other),
            device_id_type=MESH,
        )

    def result_copy(place):
        return pltpu.make_async_copy(gathered.at[place], result.at[place], result_sem.at[place])

    def send_result(step, carry):
        gather_copy(n, (n + step) % nbrs).start()
        return carry

    def await_result(step, carry):
        other = (n + step) % nbrs
        gather_copy(other, other).wait_recv()
        result_copy(other).start()
        return carry

    def await_part(step, carry):
        other = (n + step) % nbrs
        part_copy(other, other).wait_recv()
        return carry

    def await_mirror(other, carry):
        mirror_copy(other, other).wait_recv()
        return carry

    def reduce_slot():
        lax.fori_loop(1, nbrs, await_part, 0)
        lax.fori_loop(0, nbrs, await_mirror, 0)
        total = parts_in[0]
        other_tile = mirror_in[0]
        for other in range(1, nbrs):
            total = total + parts_in[other]
            other_tile = other_tile + mirror_in[other]
        turned_tile = pltpu.roll(other_tile, G, 1)
        square = jnp.concatenate(
            [other_tile, turned_tile, other_tile, turned_tile], axis=0
        ).T
        flipped = jnp.where(low_half, square[0:half], square[half:G])
        link = links[0, n].astype(jnp.float32)
        gathered[n, 0:half, :] = link * (total[0:half] + flipped)
        gathered[n, half:, :] = total[half:]
        lax.fori_loop(1, nbrs, send_result, 0)

    def one_part(more, step, carry):
        slot = in_order(step)
        panel_copy((slot + slots // 2) % slots, slot).wait_recv()
        parts_out[slot, 0:half, :] = tile_part(slot, rows[step % 2])
        if more:
            own_rows(step + 1)
        mirror_copy(slot, n).start()

        @pl.when(slot != n)
        def _():
            part_copy(slot, n).start()

        @pl.when(slot == n)
        def _():
            parts_in[n] = parts_out[n]

        return carry

    own_rows(0)
    lax.fori_loop(0, slots - 1, functools.partial(one_part, True), 0)
    one_part(False, slots - 1, 0)

    reduce_slot()

    result_copy(n).start()
    lax.fori_loop(1, nbrs, await_result, 0)
    @pl.when(n < nbrs - 1)
    def _():
        halo_up.wait_send()

    @pl.when(n > 0)
    def _():
        halo_down.wait_send()

    for slot in range(slots):
        panel_copy(slot, (slot + slots // 2) % slots).wait_send()

    def await_sends(step, carry):
        other = (n + step) % nbrs
        part_copy(other, n).wait_send()
        mirror_copy(other, n).wait_send()
        gather_copy(n, other).wait_send()
        return carry

    lax.fori_loop(1, nbrs, await_sends, 0)
    for place in range(nbrs):
        result_copy(place).wait()
    mirror_copy(n, n).wait_send()


def unpack(packed, diag_out, coup_out):
    nbrs = packed.shape[0]
    half = G // 2
    share = half // nbrs
    for other in range(nbrs):
        value = packed[other]
        turned = pltpu.roll(value, G, 1)
        coup_out[0, other, 0:half, :] = value[0:half, 0:G]
        coup_out[0, other, half:G, :] = turned[0:half, 0:G]
        at = other * share
        diag_out[0, at:at + share, :] = value[half:half + share, 0:G]
        diag_out[0, half + at:half + at + share, :] = turned[half:half + share, 0:G]


def body(subs, nbrs, eigenvectors, stencil_coef, layout, band_links, send_rows, receive_rows):
    _, vectors, cells = eigenvectors.shape
    slots, entries = send_rows.shape[1:]
    pairs = entries // 2
    padded = cells + 2 * PLANE
    half = G // 2
    anywhere = pl.BlockSpec(memory_space=pl.ANY)
    vmem = pl.BlockSpec(memory_space=pltpu.VMEM)
    bf16, f32 = jnp.bfloat16, jnp.float32
    dma = pltpu.SemaphoreType.DMA
    packed = pl.pallas_call(
        functools.partial(kernel, subs, nbrs, slots, cells),
        out_shape=jax.ShapeDtypeStruct((nbrs, half + 8, LANES), f32),
        in_specs=[anywhere] * 6,
        out_specs=anywhere,
        scratch_shapes=[
            pltpu.VMEM((vectors, padded), bf16),
            pltpu.VMEM((padded // LANES, vectors, LANES), f32),
            pltpu.VMEM((padded // PLANE * HALF_TILES, vectors, LANES), f32),
            pltpu.VMEM((cells, LANES), f32),
            pltpu.VMEM((cells, LANES), f32),
            pltpu.VMEM((cells // LANES // 2, vectors, LANES), f32),
            pltpu.VMEM((27, cells // LANES, LANES), f32),
            pltpu.VMEM((27, cells // LANES, LANES), f32),
            pltpu.VMEM((2, pairs, LANES), f32),
            pltpu.VMEM((slots, pairs, LANES), bf16),
            pltpu.VMEM((slots, pairs, LANES), bf16),
            pltpu.VMEM((vectors, cells), bf16),
            pltpu.VMEM((G, LANES), f32),
            pltpu.VMEM((nbrs, half + 8, LANES), f32),
            pltpu.VMEM((nbrs, half + 8, LANES), f32),
            pltpu.VMEM((nbrs, half, LANES), f32),
            pltpu.VMEM((nbrs, half + 8, LANES), f32),
            pltpu.SMEM(layout.shape, jnp.int32),
            pltpu.SMEM(band_links.shape, jnp.int32),
            pltpu.SMEM(send_rows.shape, jnp.int32),
            pltpu.SMEM(receive_rows.shape, jnp.int32),
            dma((6,)), dma((2,)), dma((2,)), dma((slots,)), dma((slots,)),
            dma((nbrs,)), dma((nbrs,)), dma((slots,)), dma((nbrs,)), dma((nbrs,)), dma((nbrs,)),
            dma((nbrs,)),
        ],
        compiler_params=pltpu.CompilerParams(
            collective_id=0, has_side_effects=True, vmem_limit_bytes=56 << 20
        ),
    )(eigenvectors, stencil_coef.reshape(27, cells // LANES, LANES), layout, band_links, send_rows, receive_rows)
    return pl.pallas_call(
        unpack,
        out_shape=(
            jax.ShapeDtypeStruct((1, G, G), f32),
            jax.ShapeDtypeStruct((1, slots, G, G), f32),
        ),
        in_specs=[vmem],
        out_specs=(vmem, vmem),
    )(packed)


def solution(mesh):
    in_specs = (
        P("sub", None, "nbr"),
        P("sub", None, "nbr"),
        P(),
        P("sub", None),
        P("sub", None, "nbr"),
        P("sub", None, "nbr"),
    )
    out_specs = (P("sub", None, None), P("sub", None, None, None))
    return jax.shard_map(
        functools.partial(body, mesh.shape["sub"], mesh.shape["nbr"]),
        mesh=mesh, in_specs=in_specs, out_specs=out_specs, check_vma=False,
    )
```

```python
import functools

import jax
import jax.numpy as jnp
from jax import lax
from jax.experimental import pallas as pl
from jax.experimental.pallas import tpu as pltpu
from jax.sharding import PartitionSpec as P

MESH = pl.DeviceIdType.MESH
G = 64
LANES = 128
PLANE = G * G
PLANE_TILES = PLANE // LANES
WIDE = 256
HALF_TILES = PLANE_TILES + 1
PREPARE_UNROLL = 8
HALO_UNROLL = 4
STENCIL_UNROLL = 4
NT = (((1,), (1,)), ((), ()))
TN = (((0,), (0,)), ((), ()))


def slot_offset(slot):
    back = slot // 4
    return (slot + 1) * (1 - back) + (3 - slot) * back


def kernel(
    subs, nbrs, slots, cells,
    eig, coef, layout_in, links_in, send_in, recv_in,
    result,
    field, wide_field, half_field, table, applied_table, begun_sums, weights, shifted, rows, panel, arrived,
    applied, diagonal, parts_out, parts_in, mirror_in, diagonal_in, gathered,
    layout, links, send, recv,
    load_sem, halo_send, halo_recv, panel_send, panel_recv,
    part_send, part_recv, mirror_send, mirror_recv, gather_send, gather_recv, result_sem, diagonal_send, diagonal_recv,
):
    s = lax.axis_index("sub")
    n = lax.axis_index("nbr")
    pairs = panel.shape[1]
    vectors = field.shape[0]
    tiles = cells // LANES
    chunks = pairs // LANES

    def in_order(step):
        pair = step // 2
        late = pair // 2
        return (1 - pair) * (1 - late) + pair * late + step % 2 * (slots // 2)

    def neighbour(slot):
        return (s + slot_offset(slot) + subs) % subs

    load_field = pltpu.make_async_copy(
        eig.at[0], field.at[:, pl.ds(PLANE, cells)], load_sem.at[0]
    )
    load_weights = pltpu.make_async_copy(coef, weights, load_sem.at[1])
    load_scalars = [
        pltpu.make_async_copy(source, target, load_sem.at[2 + i])
        for i, (source, target) in enumerate(
            ((send_in, send), (recv_in, recv), (layout_in, layout), (links_in, links))
        )
    ]
    load_field.start()
    load_scalars[0].start()
    load_weights.start()
    for load in load_scalars[1:]:
        load.start()

    barrier = pltpu.get_barrier_semaphore()
    for slot in range(slots):
        pl.semaphore_signal(
            barrier, inc=1, device_id=(neighbour(slot), n), device_id_type=MESH
        )
    for step in range(1, nbrs):
        pl.semaphore_signal(
            barrier, inc=1, device_id=(s, (n + step) % nbrs), device_id_type=MESH
        )
    for other in range(nbrs):
        pl.semaphore_signal(
            barrier, inc=1, device_id=(neighbour(n), other), device_id_type=MESH
        )

    lane = lax.broadcasted_iota(jnp.int32, (1, LANES), 1)
    low_half = lane < G
    diagonal[...] = jnp.zeros_like(diagonal)

    pl.semaphore_wait(barrier, 2 * slots + nbrs - 1)

    last = field.shape[1] - PLANE
    halo_up = pltpu.make_async_remote_copy(
        src_ref=eig.at[0, :, pl.ds(cells - PLANE, PLANE)],
        dst_ref=field.at[:, pl.ds(0, PLANE)],
        send_sem=halo_send.at[0],
        recv_sem=halo_recv.at[0],
        device_id=(s, (n + 1) % nbrs),
        device_id_type=MESH,
    )
    halo_down = pltpu.make_async_remote_copy(
        src_ref=eig.at[0, :, pl.ds(0, PLANE)],
        dst_ref=field.at[:, pl.ds(last, PLANE)],
        send_sem=halo_send.at[1],
        recv_sem=halo_recv.at[1],
        device_id=(s, (n + nbrs - 1) % nbrs),
        device_id_type=MESH,
    )

    @pl.when(n < nbrs - 1)
    def _():
        halo_up.start()

    @pl.when(n > 0)
    def _():
        halo_down.start()

    def turn(block, target, place):
        target[pl.ds(place, LANES), :] = jnp.concatenate([block, block], axis=0).T

    def gather_some(index_ref, source, slot, target, first, count):
        views = [index_ref.at[0, slot, pl.ds(k * LANES, LANES)] for k in range(2 * chunks)]
        for u in range(first, first + count):
            for k in range(chunks):
                target[pl.ds(k * LANES + u, 1), :] = jnp.where(
                    low_half,
                    source[pl.ds(views[k][u], 1), :],
                    source[pl.ds(views[k + chunks][u], 1), :],
                )

    column = lane % G
    blank = jnp.zeros((vectors, LANES), jnp.float32)

    def widen(value, source, tile, before):
        turned = pltpu.roll(value, G, 1)
        wide_field[source] = value
        half_field[tile] = jnp.where(low_half, before, turned)
        return turned

    def wide_tile(source):
        begin = pl.multiple_of(source * LANES, LANES)
        return field[:, pl.ds(begin, LANES)].astype(jnp.float32)

    def prepare(i, before):
        tile = i * PREPARE_UNROLL
        before = jnp.where(tile % PLANE_TILES == 0, blank, before)
        place = (tile // PLANE_TILES + 1) * HALF_TILES + tile % PLANE_TILES
        for u in range(PREPARE_UNROLL):
            value = wide_tile(tile + u + PLANE_TILES)
            turn(value, table, pl.multiple_of((tile + u) * LANES, LANES))
            before = widen(value, tile + u + PLANE_TILES, place + u, before)
        half_field[place + PREPARE_UNROLL] = jnp.where(low_half, before, 0.0)
        at = pl.ds(pl.multiple_of(tile, PREPARE_UNROLL), PREPARE_UNROLL)
        for k in range(27):
            w = weights[layout[k], at, :]
            if k % 3 == 0:
                w = jnp.where(column != G - 1, pltpu.roll(w, LANES - 1, 1), 0.0)
            if k % 3 == 2:
                w = jnp.where(column != 0, pltpu.roll(w, 1, 1), 0.0)
            shifted[k, at, :] = w
        return before

    load_field.wait()
    load_weights.wait()
    for load in load_scalars:
        load.wait()
    lax.fori_loop(0, tiles // PREPARE_UNROLL, prepare, blank)

    def panel_copy(slot, landing):
        return pltpu.make_async_remote_copy(
            src_ref=panel.at[slot],
            dst_ref=arrived.at[landing],
            send_sem=panel_send.at[slot],
            recv_sem=panel_recv.at[landing],
            device_id=(neighbour(slot), n),
            device_id_type=MESH,
        )

    def take_halos():
        @pl.when(n > 0)
        def _():
            halo_up.wait_recv()

        @pl.when(n == 0)
        def _():
            field[:, pl.ds(0, PLANE)] = jnp.zeros((vectors, PLANE), jnp.bfloat16)

        @pl.when(n < nbrs - 1)
        def _():
            halo_down.wait_recv()

        @pl.when(n == nbrs - 1)
        def _():
            field[:, pl.ds(last, PLANE)] = jnp.zeros((vectors, PLANE), jnp.bfloat16)

        halo_planes = (0, field.shape[1] // PLANE - 1)

        def widen_halo(i, carry):
            carry = list(carry)
            for which, plane in enumerate(halo_planes):
                for u in range(HALO_UNROLL):
                    t = i * HALO_UNROLL + u
                    source = plane * PLANE_TILES + t
                    carry[which] = widen(
                        wide_tile(source), source, plane * HALF_TILES + t, carry[which]
                    )
            return tuple(carry)

        ends = lax.fori_loop(0, PLANE_TILES // HALO_UNROLL, widen_halo, (blank, blank))
        for plane, end in zip(halo_planes, ends):
            half_field[plane * HALF_TILES + PLANE_TILES] = jnp.where(low_half, end, 0.0)
    def stencil_tile(t, planes=(0, 1, 2), begun=False, keep=False):
        plane = t // PLANE_TILES
        place = t % begun_sums.shape[0]
        scaled = {
            k: jnp.broadcast_to(shifted[k, pl.ds(t, 1), :], (8, LANES))
            for a in planes
            for k in range(9 * a, 9 * a + 9)
        }
        for pair in range(vectors // 16):
            halves = []
            for side in range(2):
                at = pl.ds(pair * 16 + side * 8, 8)
                sums = [None, None, None]
                for a in planes:
                    for b in range(3):
                        if b == 1:
                            x = wide_field[t + a * PLANE_TILES, at, :]
                        else:
                            x = half_field[t + plane + a * HALF_TILES + b // 2, at, :]
                        for c in range(3):
                            term = scaled[9 * a + 3 * b + c] * x
                            sums[c] = term if sums[c] is None else sums[c] + term
                value = sums[1] + pltpu.roll(sums[0], 1, 1) + pltpu.roll(sums[2], LANES - 1, 1)
                if begun:
                    value = value + begun_sums[place, at, :]
                if keep:
                    begun_sums[place, at, :] = value
                halves.append(value)
            if not keep:
                applied[pl.ds(pair * 16, 16), pl.ds(pl.multiple_of(t * LANES, LANES), LANES)] = (
                    jnp.concatenate(halves, axis=0).astype(jnp.bfloat16)
                )

    def use_applied(first_tile):
        for u in range(STENCIL_UNROLL):
            begin = pl.multiple_of((first_tile + u) * LANES, LANES)
            turn(applied[:, pl.ds(begin, LANES)].astype(jnp.float32), applied_table, begin)
        for u in range(STENCIL_UNROLL // 2):
            begin = pl.multiple_of((first_tile + 2 * u) * LANES, WIDE)
            block = applied[:, pl.ds(begin, WIDE)]
            diagonal[...] += lax.dot_general(
                field[:, pl.ds(pl.multiple_of(PLANE + begin, WIDE), WIDE)],
                jnp.concatenate([block, block], axis=0),
                NT, preferred_element_type=jnp.float32,
            )

    def block(step):
        return (step * STENCIL_UNROLL + PLANE_TILES) % tiles

    blocks = tiles // STENCIL_UNROLL
    applied[:, pl.ds(PLANE, STENCIL_UNROLL * LANES)] = jnp.zeros(
        (vectors, STENCIL_UNROLL * LANES), jnp.bfloat16
    )
    def one_slot(step, carry):
        slot = in_order(step)
        use_applied(block(jnp.maximum(step - 1, 0)))
        count = LANES // STENCIL_UNROLL
        for u in range(STENCIL_UNROLL):
            gather_some(send, table, slot, rows.at[0], u * count, count)
            stencil_tile(block(step) + u)
        panel[slot] = rows[0].astype(jnp.bfloat16)
        panel_copy(slot, (slot + slots // 2) % slots).start()
        return carry

    def later_block(step, carry):
        use_applied(block(step - 1))
        for u in range(STENCIL_UNROLL):
            stencil_tile(block(step) + u)
        return carry

    lax.fori_loop(0, slots, one_slot, 0)
    lax.fori_loop(slots, blocks // 2, later_block, 0)

    def begin_block(planes, step, carry):
        for u in range(STENCIL_UNROLL):
            stencil_tile(block(step) + u, planes, keep=True)
        return carry

    def finish_block(planes, step, carry):
        use_applied(block(step - 1))
        for u in range(STENCIL_UNROLL):
            stencil_tile(block(step) + u, planes, begun=True)
        return carry

    turn_point = blocks // 2 + blocks // 4
    lax.fori_loop(blocks // 2, turn_point, functools.partial(begin_block, (0, 1)), 0)
    lax.fori_loop(turn_point, blocks, functools.partial(begin_block, (1, 2)), 0)
    take_halos()
    lax.fori_loop(blocks // 2, turn_point, functools.partial(finish_block, (2,)), 0)
    lax.fori_loop(turn_point, blocks, functools.partial(finish_block, (0,)), 0)
    use_applied(block(blocks - 1))

    half = G // 2
    diagonal_in[n] = jnp.where(low_half, diagonal[0:half, :], diagonal[half:G, :])

    def diagonal_copy(place, other):
        return pltpu.make_async_remote_copy(
            src_ref=diagonal_in.at[place],
            dst_ref=diagonal_in.at[place],
            send_sem=diagonal_send.at[other],
            recv_sem=diagonal_recv.at[place],
            device_id=(s, other),
            device_id_type=MESH,
        )

    def send_diagonal(step, carry):
        diagonal_copy(n, (n + step) % nbrs).start()
        return carry

    def await_diagonal(step, carry):
        other = (n + step) % nbrs
        diagonal_copy(other, other).wait_recv()
        return carry

    lax.fori_loop(1, nbrs, send_diagonal, 0)

    def own_rows(step):
        gather_some(recv, applied_table, in_order(step), rows.at[step % 2], 0, LANES)

    def tile_part(slot, own):
        product = lax.dot_general(
            own.astype(jnp.bfloat16), arrived[slot], TN, preferred_element_type=jnp.float32
        )
        tile = product[0:G] + pltpu.roll(product[G:2 * G], G, 1)
        return jnp.where(low_half, tile[0:half], pltpu.roll(tile[half:G], G, 1))

    def part_copy(other, me):
        return pltpu.make_async_remote_copy(
            src_ref=parts_out.at[other],
            dst_ref=parts_in.at[me],
            send_sem=part_send.at[other],
            recv_sem=part_recv.at[me],
            device_id=(s, other),
            device_id_type=MESH,
        )

    def mirror_copy(slot, me):
        return pltpu.make_async_remote_copy(
            src_ref=parts_out.at[slot],
            dst_ref=mirror_in.at[me],
            send_sem=mirror_send.at[slot],
            recv_sem=mirror_recv.at[me],
            device_id=(neighbour(slot), (slot + slots // 2) % slots),
            device_id_type=MESH,
        )

    def gather_copy(place, other):
        return pltpu.make_async_remote_copy(
            src_ref=gathered.at[place],
            dst_ref=gathered.at[place],
            send_sem=gather_send.at[other],
            recv_sem=gather_recv.at[place],
            device_id=(s, other),
            device_id_type=MESH,
        )

    def result_copy(place):
        return pltpu.make_async_copy(gathered.at[place], result.at[place], result_sem.at[place])

    def send_result(step, carry):
        gather_copy(n, (n + step) % nbrs).start()
        return carry

    def await_result(step, carry):
        other = (n + step) % nbrs
        gather_copy(other, other).wait_recv()
        result_copy(other).start()
        return carry

    def await_part(step, carry):
        other = (n + step) % nbrs
        part_copy(other, other).wait_recv()
        return carry

    def await_mirror(other, carry):
        mirror_copy(other, other).wait_recv()
        return carry

    def reduce_slot():
        lax.fori_loop(1, nbrs, await_part, 0)
        lax.fori_loop(0, nbrs, await_mirror, 0)
        total = parts_in[0]
        other_tile = mirror_in[0]
        for other in range(1, nbrs):
            total = total + parts_in[other]
            other_tile = other_tile + mirror_in[other]
        turned_tile = pltpu.roll(other_tile, G, 1)
        square = jnp.concatenate(
            [other_tile, turned_tile, other_tile, turned_tile], axis=0
        ).T
        flipped = jnp.where(low_half, square[0:half], square[half:G])
        link = links[0, n].astype(jnp.float32)
        gathered[n] = link * (total + flipped)
        lax.fori_loop(1, nbrs, send_result, 0)

    def one_part(more, step, carry):
        slot = in_order(step)
        panel_copy((slot + slots // 2) % slots, slot).wait_recv()
        parts_out[slot] = tile_part(slot, rows[step % 2])
        if more:
            own_rows(step + 1)
        mirror_copy(slot, n).start()

        @pl.when(slot != n)
        def _():
            part_copy(slot, n).start()

        @pl.when(slot == n)
        def _():
            parts_in[n] = parts_out[n]

        return carry

    own_rows(0)
    lax.fori_loop(0, slots - 1, functools.partial(one_part, True), 0)
    one_part(False, slots - 1, 0)

    lax.fori_loop(1, nbrs, await_diagonal, 0)
    diagonal_sum = diagonal_in[0]
    for other in range(1, nbrs):
        diagonal_sum = diagonal_sum + diagonal_in[other]
    gathered[nbrs] = diagonal_sum
    result_copy(nbrs).start()
    reduce_slot()

    result_copy(n).start()
    lax.fori_loop(1, nbrs, await_result, 0)
    @pl.when(n < nbrs - 1)
    def _():
        halo_up.wait_send()

    @pl.when(n > 0)
    def _():
        halo_down.wait_send()

    for slot in range(slots):
        panel_copy(slot, (slot + slots // 2) % slots).wait_send()

    def await_sends(step, carry):
        other = (n + step) % nbrs
        part_copy(other, n).wait_send()
        diagonal_copy(n, other).wait_send()
        mirror_copy(other, n).wait_send()
        gather_copy(n, other).wait_send()
        return carry

    lax.fori_loop(1, nbrs, await_sends, 0)
    for place in range(nbrs + 1):
        result_copy(place).wait()
    mirror_copy(n, n).wait_send()


def unpack(packed, diag_out, coup_out):
    half = G // 2
    for slot in range(packed.shape[0]):
        value = packed[slot]
        turned = pltpu.roll(value, G, 1)
        last = slot == packed.shape[0] - 1
        target = diag_out.at[0] if last else coup_out.at[0, slot]
        target[0:half, :] = value[:, 0:G]
        target[half:G, :] = turned[:, 0:G]


def body(subs, nbrs, eigenvectors, stencil_coef, layout, band_links, send_rows, receive_rows):
    _, vectors, cells = eigenvectors.shape
    slots, entries = send_rows.shape[1:]
    pairs = entries // 2
    padded = cells + 2 * PLANE
    half = G // 2
    anywhere = pl.BlockSpec(memory_space=pl.ANY)
    vmem = pl.BlockSpec(memory_space=pltpu.VMEM)
    bf16, f32 = jnp.bfloat16, jnp.float32
    dma = pltpu.SemaphoreType.DMA
    packed = pl.pallas_call(
        functools.partial(kernel, subs, nbrs, slots, cells),
        out_shape=jax.ShapeDtypeStruct((nbrs + 1, half, LANES), f32),
        in_specs=[anywhere] * 6,
        out_specs=anywhere,
        scratch_shapes=[
            pltpu.VMEM((vectors, padded), bf16),
            pltpu.VMEM((padded // LANES, vectors, LANES), f32),
            pltpu.VMEM((padded // PLANE * HALF_TILES, vectors, LANES), f32),
            pltpu.VMEM((cells, LANES), f32),
            pltpu.VMEM((cells, LANES), f32),
            pltpu.VMEM((cells // LANES // 2, vectors, LANES), f32),
            pltpu.VMEM((27, cells // LANES, LANES), f32),
            pltpu.VMEM((27, cells // LANES, LANES), f32),
            pltpu.VMEM((2, pairs, LANES), f32),
            pltpu.VMEM((slots, pairs, LANES), bf16),
            pltpu.VMEM((slots, pairs, LANES), bf16),
            pltpu.VMEM((vectors, cells), bf16),
            pltpu.VMEM((G, LANES), f32),
            pltpu.VMEM((nbrs, half, LANES), f32),
            pltpu.VMEM((nbrs, half, LANES), f32),
            pltpu.VMEM((nbrs, half, LANES), f32),
            pltpu.VMEM((nbrs, half, LANES), f32),
            pltpu.VMEM((nbrs + 1, half, LANES), f32),
            pltpu.SMEM(layout.shape, jnp.int32),
            pltpu.SMEM(band_links.shape, jnp.int32),
            pltpu.SMEM(send_rows.shape, jnp.int32),
            pltpu.SMEM(receive_rows.shape, jnp.int32),
            dma((6,)), dma((2,)), dma((2,)), dma((slots,)), dma((slots,)),
            dma((nbrs,)), dma((nbrs,)), dma((slots,)), dma((nbrs,)), dma((nbrs,)), dma((nbrs,)),
            dma((nbrs + 1,)), dma((nbrs,)), dma((nbrs,)),
        ],
        compiler_params=pltpu.CompilerParams(
            collective_id=0, has_side_effects=True, vmem_limit_bytes=56 << 20
        ),
    )(eigenvectors, stencil_coef.reshape(27, cells // LANES, LANES), layout, band_links, send_rows, receive_rows)
    return pl.pallas_call(
        unpack,
        out_shape=(
            jax.ShapeDtypeStruct((1, G, G), f32),
            jax.ShapeDtypeStruct((1, slots, G, G), f32),
        ),
        in_specs=[vmem],
        out_specs=(vmem, vmem),
    )(packed)


def solution(mesh):
    in_specs = (
        P("sub", None, "nbr"),
        P("sub", None, "nbr"),
        P(),
        P("sub", None),
        P("sub", None, "nbr"),
        P("sub", None, "nbr"),
    )
    out_specs = (P("sub", None, None), P("sub", None, None, None))
    return jax.shard_map(
        functools.partial(body, mesh.shape["sub"], mesh.shape["nbr"]),
        mesh=mesh, in_specs=in_specs, out_specs=out_specs, check_vma=False,
    )
```
